32 devices in a mesh: req: 4 (over z), cp: 8 (over y, x, core).
Axes of the slice: x: 2, y: 2, z: 4, core: 2. Of those that a mesh axis runs over, the one named last changes fastest.
Arguments:
- hidden: bfloat16 [4, 256, 8192], P('req', 'cp'), may hold values from -8 to 8
- residual: bfloat16 [4, 256, 8192], P('req', 'cp'), may hold values from -6 to 6
- w_query: bfloat16 [8192, 8192], P(None, 'cp'), may hold values from -0.0625 to 0.0625
- w_keyval: bfloat16 [8192, 2048], P('cp'), may hold values from -0.0625 to 0.0625
- w_out: bfloat16 [8192, 8192], P('cp'), may hold values from -0.375 to 0.375
- kv_pool: bfloat16 [96, 128, 2048], P('req', 'cp'), may hold values from -6 to 6
- prefix_len: int32 [4], replicated, may hold values from 1 to 3072, as said below
- hit_holder: int32 [4, 24], replicated, may hold values from 0 to 3, as said below
- hit_slot: int32 [4, 24], replicated, may hold values from 0 to 23, as said below
- owner: int32 [4, 2], replicated, may hold values from 0 to 3, as said below
Outputs:
- layer_out: bfloat16 [4, 256, 8192], P('req', 'cp')
- new_cache: bfloat16 [4, 4, 128, 2048], P('req', None, 'cp')
The draws below stay inside these ranges and needn't reach their ends.
Inputs may be any that keep to these rules, and one draw needn't show every extreme that they name: `hit_holder`: no holder holds more than 12 of one request's hits, and for every request one holder holds exactly 12. `hit_slot`: the hits of one request name distinct slots. `prefix_len`: some request has the longest prefix and some the shortest. No owner receives more than 1 new blocks of one request, and every request sends exactly 1 to one owner.
All inputs are finite; a program needn't handle non-finite values.
Results may differ from the reference program's by a relative error of at most 0.013.
Values may be sent and summed in bfloat16 or wider, within the bound.
No kernel may reach another device: no remote copies, remote signals or barrier semaphores. Data moves between devices by JAX's collectives and lax.ppermute only.
A program may use at most 192 MiB of HBM per device.

```python
import math
import jax
import jax.numpy as jnp
from jax import lax

D = 8192
HQ = 64
KVH = 8
HD = 128
BLK = 128
PB = 24
REQS = 4
STRETCH = 256
NB = 2
CAP = 12
CAP2 = 1
POOL = 24
N_CP = 8


def cache_hits(key):

    def per_request(subkey):
        parts = jax.random.split(subkey, 4)
        busiest = jax.random.randint(parts[0], (), 0, REQS, dtype=jnp.int32)
        others = jax.random.randint(parts[1], (PB - CAP,), 0, REQS - 1, dtype=jnp.int32)
        others = others + (others >= busiest).astype(jnp.int32)
        holders = jnp.concatenate([jnp.full((CAP,), busiest, jnp.int32), others])
        holders = holders[jax.random.permutation(parts[2], PB)]
        slot_ids = jax.random.permutation(parts[3], POOL)[:PB].astype(jnp.int32)
        return (holders.astype(jnp.int32), slot_ids)
    return jax.vmap(per_request)(jax.random.split(key, REQS))


def draw_hit_holder(key, part):
    return cache_hits(key)[0]


def draw_hit_slot(key, part):
    return cache_hits(key)[1]


def draw_prefix_len(key, part):
    key = jax.random.fold_in(key, 7)
    parts = jax.random.split(key, 3)
    lengths = jax.random.randint(parts[0], (REQS,), 1, PB * BLK + 1, dtype=jnp.int32)
    longest = jax.random.randint(parts[1], (), 0, REQS, dtype=jnp.int32)
    shortest = (longest + 1 + jax.random.randint(parts[2], (), 0, REQS - 1, dtype=jnp.int32)) % REQS
    return lengths.at[longest].set(PB * BLK).at[shortest].set(1)


def draw_owner(key, part):
    key = jax.random.fold_in(key, 5)

    def per_request(subkey):
        parts = jax.random.split(subkey, 3)
        busiest = jax.random.randint(parts[0], (), 0, REQS, dtype=jnp.int32)
        others = jax.random.randint(parts[1], (NB - CAP2,), 0, REQS - 1, dtype=jnp.int32)
        others = others + (others >= busiest).astype(jnp.int32)
        owners = jnp.concatenate([jnp.full((CAP2,), busiest, jnp.int32), others])
        return owners[jax.random.permutation(parts[2], NB)].astype(jnp.int32)
    return jax.vmap(per_request)(jax.random.split(key, REQS))


def draw_hidden(key, part):
    key = jax.random.fold_in(key, 11)
    values = jnp.clip(jax.random.normal(key, (REQS, STRETCH, D), jnp.float32), -6.0, 6.0)
    return values.astype(jnp.bfloat16)


def block_levels(own_key, dims, cuts, low, largest):
    loudness = 1.0
    for axis_at, blocks in cuts:
        steps = jax.random.uniform(jax.random.fold_in(jax.random.fold_in(own_key, 6), axis_at), (blocks,), jnp.float32, low / len(cuts), largest / len(cuts))
        loudness = loudness * jnp.repeat(jnp.exp(steps), dims[axis_at] // blocks).reshape((-1,) + (1,) * (len(dims) - 1 - axis_at))
    return loudness


def noise(rng, extent, spread, most, pieces=(), held_as=jnp.bfloat16):
    array = jax.random.normal(rng, extent, jnp.float32) * spread
    if len(pieces) > 0:
        array = block_levels(rng, extent, pieces, -0.22, 0.18) * array
    return jnp.clip(array, min=-most, max=most).astype(held_as)


def setup_inputs(seed: int = 0) -> dict:
    seeds = jax.random.split(jax.random.key(seed), 11)
    return {
        "hidden": draw_hidden(jax.random.fold_in(seeds[10], 71), 0),
        "residual": noise(seeds[1], (REQS, STRETCH, D), 1.0, 6.0, ((0, 4), (1, 8))),
        "w_query": noise(seeds[2], (D, HQ * HD), D ** -0.5, 0.0625, ((1, 8),)),
        "w_keyval": noise(seeds[3], (D, 2 * KVH * HD), D ** -0.5, 0.0625, ((0, 8),)),
        "w_out": noise(seeds[4], (HQ * HD, D), (HQ * HD // 32) ** -0.5, 0.375, ((0, 8),)),
        "kv_pool": noise(seeds[5], (REQS * POOL, BLK, 2 * KVH * HD), 1.0, 6.0, ((0, 4), (1, 8))),
        "prefix_len": draw_prefix_len(jax.random.fold_in(seeds[10], 71), 0),
        "hit_holder": draw_hit_holder(jax.random.fold_in(seeds[10], 71), 0),
        "hit_slot": draw_hit_slot(jax.random.fold_in(seeds[10], 71), 0),
        "owner": draw_owner(jax.random.fold_in(seeds[10], 71), 0),
    }


def frequencies(width):
    half_width = width // 2
    base_freq = jnp.power(jnp.float32(500000.0), -jnp.arange(half_width, dtype=jnp.float32) * (2.0 / width))
    wavelength = (2.0 * math.pi) / base_freq
    blended = (8192.0 / wavelength - 1.0) / 3.0
    middle = (1.0 - blended) * base_freq / 8.0 + blended * base_freq
    return jnp.where(wavelength < 2048.0, base_freq, jnp.where(wavelength > 8192.0, base_freq / 8.0, middle))


def rotate(values, positions):
    half_width = values.shape[-1] // 2
    inverse = frequencies(values.shape[-1])
    angles = positions.astype(jnp.float32)[:, None] * inverse[None, :]
    cosine = jnp.cos(angles)[:, None, :]
    sine_table = jnp.sin(angles)[:, None, :]
    first_half = values[..., :half_width]
    second = values[..., half_width:]
    return jnp.concatenate([first_half * cosine - second * sine_table, second * cosine + first_half * sine_table], axis=-1)


def fresh_keyvals(summed, positions):
    row_count = summed.shape[0]
    key_width = KVH * HD
    rotated = rotate(summed[:, :key_width].reshape(row_count, KVH, HD), positions).reshape(row_count, key_width)
    return jnp.concatenate([rotated, summed[:, key_width:]], axis=1).astype(jnp.bfloat16)


def reference(hidden, residual, w_query, w_keyval, w_out, kv_pool, prefix_len, hit_holder, hit_slot, owner):
    group_size = HQ // KVH
    per_device = HQ // N_CP
    key_width = KVH * HD
    span = PB * BLK
    score_scale = HD ** -0.5
    outputs = []
    new_cache = jnp.zeros((REQS, REQS * CAP2, BLK, 2 * key_width), jnp.bfloat16)
    for request in range(REQS):
        tokens = hidden[request]
        length = prefix_len[request]
        positions = length + jnp.arange(STRETCH, dtype=jnp.int32)
        queries = rotate(jnp.dot(tokens, w_query, preferred_element_type=jnp.float32).reshape(STRETCH, HQ, HD), positions).astype(jnp.bfloat16)
        fresh_kv = fresh_keyvals(jnp.dot(tokens, w_keyval, preferred_element_type=jnp.float32), positions)
        pool_rows = (hit_holder[request] * POOL + hit_slot[request]).astype(jnp.int32)
        prefix = kv_pool[pool_rows].reshape(span, 2 * key_width)
        stacked = jnp.concatenate([prefix, fresh_kv], axis=0)
        key_index = jnp.arange(span + STRETCH, dtype=jnp.int32)[None, :]
        query_index = jnp.arange(STRETCH, dtype=jnp.int32)[:, None]
        visible = jnp.where(key_index < span, key_index < length, key_index - span <= query_index)

        def one_head(head_index):
            kv_head = (head_index // group_size).astype(jnp.int32)
            head_query = lax.dynamic_index_in_dim(queries, head_index, 1, keepdims=False)
            head_keys = lax.dynamic_slice_in_dim(stacked, kv_head * HD, HD, 1)
            head_values = lax.dynamic_slice_in_dim(stacked, key_width + kv_head * HD, HD, 1)
            scores = jnp.dot(head_query, head_keys.T, preferred_element_type=jnp.float32) * score_scale
            scores = jnp.where(visible, scores, -1e30)
            row_peak = jnp.max(scores, axis=1, keepdims=True)
            weights = jnp.exp(scores - row_peak)
            denominator = jnp.sum(weights, axis=1, keepdims=True)
            mixed_heads = jnp.dot(weights.astype(jnp.bfloat16), head_values, preferred_element_type=jnp.float32) / denominator
            return mixed_heads.astype(jnp.bfloat16)

        heads_out = lax.map(one_head, jnp.arange(HQ, dtype=jnp.int32))
        attended = jnp.transpose(heads_out, (1, 0, 2)).reshape(STRETCH, HQ * HD)

        def add_share(step_index, carry):
            row_start = (step_index * per_device * HD).astype(jnp.int32)
            partial_value = jnp.dot(lax.dynamic_slice_in_dim(attended, row_start, per_device * HD, 1),
                              lax.dynamic_slice_in_dim(w_out, row_start, per_device * HD, 0),
                              preferred_element_type=jnp.float32)
            rounded = lax.optimization_barrier(partial_value.astype(jnp.bfloat16)).astype(jnp.float32)
            return carry + rounded

        projected = lax.fori_loop(0, N_CP, add_share, jnp.zeros((STRETCH, D), jnp.float32))
        outputs.append((residual[request].astype(jnp.float32) + projected).astype(jnp.bfloat16))
        blocks = fresh_kv.reshape(NB, BLK, 2 * key_width)
        for block_index in range(NB):
            target = owner[request, block_index]
            slot_index = request * CAP2 + jnp.sum((owner[request, :block_index] == target).astype(jnp.int32))
            new_cache = new_cache.at[target, slot_index].set(blocks[block_index])
    return jnp.stack(outputs), new_cache
```

```python
import functools
import math

import jax
import jax.numpy as jnp
from jax import lax
from jax.experimental import pallas as pl
from jax.experimental.pallas import tpu as pltpu
from jax.sharding import PartitionSpec as P

KVH = 8
HD = 128
BLK = 128
LOG2E = 1.4426950408889634


def frequencies(width):
    half_width = width // 2
    base_freq = jnp.power(
        jnp.float32(500000.0), -jnp.arange(half_width, dtype=jnp.float32) * (2.0 / width)
    )
    wavelength = 2.0 * math.pi / base_freq
    blended = (8192.0 / wavelength - 1.0) / 3.0
    middle = (1.0 - blended) * base_freq / 8.0 + blended * base_freq
    return jnp.where(
        wavelength < 2048.0, base_freq, jnp.where(wavelength > 8192.0, base_freq / 8.0, middle)
    )


def rope_tables(positions):
    angles = positions.astype(jnp.float32)[:, None] * frequencies(HD)[None, :]
    cosine, sine = jnp.cos(angles), jnp.sin(angles)
    return jnp.concatenate([cosine, cosine], axis=1), jnp.concatenate([-sine, sine], axis=1)


def attention_kernel(tile, chunk, stretch, length_ref, q_ref, cos_ref, sin_ref, kv_ref, fresh_ref, out_ref):
    length = length_ref[0]
    row0 = pl.program_id(1) * tile
    raw = q_ref[...]
    query = (raw * cos_ref[...] + pltpu.roll(raw, HD // 2, 1) * sin_ref[...]).astype(jnp.bfloat16)
    factor = HD ** (-0.5) * LOG2E

    def scores(keys):
        return lax.dot_general(
            query, keys, (((1,), (1,)), ((), ())), preferred_element_type=jnp.float32
        )

    def update(carry, part, values):
        peak, total, mixed = carry
        new_peak = jnp.maximum(peak, jnp.max(part, axis=1, keepdims=True))
        weights = jnp.exp2((part - new_peak) * factor)
        shrink = jnp.exp2((peak - new_peak) * factor)
        total = total * shrink + jnp.sum(weights, axis=1, keepdims=True)
        mixed = mixed * shrink + jnp.dot(
            weights.astype(jnp.bfloat16), values, preferred_element_type=jnp.float32
        )
        return new_peak, total, mixed

    carry = (
        jnp.full((tile, 1), -1e30, jnp.float32),
        jnp.zeros((tile, 1), jnp.float32),
        jnp.zeros((tile, HD), jnp.float32),
    )
    part = scores(fresh_ref[:, :HD])
    columns = lax.broadcasted_iota(jnp.int32, part.shape, 1)
    rows = lax.broadcasted_iota(jnp.int32, part.shape, 0) + row0
    carry = update(carry, jnp.where(columns <= rows, part, -1e30), fresh_ref[:, HD:])

    def whole(step, carry):
        at = pl.multiple_of(step * chunk, chunk)
        return update(carry, scores(kv_ref[pl.ds(at, chunk), :HD]), kv_ref[pl.ds(at, chunk), HD:])

    full = length // chunk
    carry = lax.fori_loop(0, full, whole, carry)

    def rest(step, carry):
        at = pl.multiple_of(step * chunk, chunk)
        part = scores(kv_ref[pl.ds(at, chunk), :HD])
        seen = lax.broadcasted_iota(jnp.int32, part.shape, 1) + at < length
        return update(carry, jnp.where(seen, part, -1e30), kv_ref[pl.ds(at, chunk), HD:])

    last = (length + chunk - 1) // chunk
    peak, total, mixed = lax.fori_loop(full, last, rest, carry)
    out_ref[...] = (mixed / total).astype(jnp.bfloat16)


def attention(length, raw_queries, cosine, sine, prefix, fresh):
    rows, width = raw_queries.shape
    tile = min(256, rows)
    chunk = 512
    return pl.pallas_call(
        functools.partial(attention_kernel, tile, chunk, rows),
        grid_spec=pltpu.PrefetchScalarGridSpec(
            num_scalar_prefetch=1,
            grid=(width // HD, rows // tile),
            in_specs=[
                pl.BlockSpec((tile, HD), lambda h, t, n: (t, h)),
                pl.BlockSpec((tile, HD), lambda h, t, n: (t, 0)),
                pl.BlockSpec((tile, HD), lambda h, t, n: (t, 0)),
                pl.BlockSpec(prefix.shape, lambda h, t, n: (0, 0)),
                pl.BlockSpec(fresh.shape, lambda h, t, n: (0, 0)),
            ],
            out_specs=pl.BlockSpec((tile, HD), lambda h, t, n: (t, h)),
        ),
        out_shape=jax.ShapeDtypeStruct((rows, width), jnp.bfloat16),
        compiler_params=pltpu.CompilerParams(vmem_limit_bytes=24 * 1024 * 1024),
        cost_estimate=pl.CostEstimate(
            flops=4 * rows * width * (prefix.shape[0] + rows),
            bytes_accessed=rows * width * 6,
            transcendentals=rows * width // HD * (prefix.shape[0] + rows),
        ),
    )(length.reshape(1), raw_queries, cosine, sine, prefix, fresh)


def swap(array, bit, count):
    return lax.ppermute(array, "cp", [(i, i ^ bit) for i in range(count)])


def pick(array, index, axis):
    return lax.dynamic_index_in_dim(array, index, axis, keepdims=False)


def add(one, two):
    return one.astype(jnp.float32) + two.astype(jnp.float32)


def scatter_sum(part, rank):
    rows, width = part.shape
    core, x, y = rank % 2, rank // 2 % 2, rank // 4
    view = part.reshape(2, 2, 2, rows // 8, width)
    got = swap(pick(view, 1 - core, 2), 1, 8)
    pair = add(pick(view, core, 2), got).astype(jnp.bfloat16)
    half = width // 2
    one, two = pair[..., :half], pair[..., half:]
    got_one = swap(pick(one, 1 - x, 1), 2, 8)
    got_two = swap(pick(two, 1 - y, 0), 4, 8)
    one = add(pick(one, x, 1), got_one)
    two = add(pick(two, y, 0), got_two)
    end_one = swap(pick(one, 1 - y, 0).astype(jnp.bfloat16), 4, 8)
    end_two = swap(pick(two, 1 - x, 0).astype(jnp.bfloat16), 2, 8)
    one = add(pick(one, y, 0), end_one)
    two = add(pick(two, x, 0), end_two)
    return jnp.concatenate([one, two], axis=1)


def local(
    hidden, residual, w_query, w_keyval, w_out, kv_pool, prefix_len, hit_holder, hit_slot, owner
):
    cp_count = lax.axis_size("cp")
    group_id = lax.axis_index("req")
    cp_rank = lax.axis_index("cp")
    tok_rows = hidden.shape[1]
    stretch_rows = tok_rows * cp_count
    slice_rows = w_keyval.shape[0]
    block_rows = kv_pool.shape[1]
    request_count = hit_holder.shape[0]
    prefix_blocks = hit_holder.shape[1]
    new_blocks = owner.shape[1]
    owner_cap = (new_blocks + 1) // 2
    holder_cap = prefix_blocks // 2
    heads_share = cp_count // KVH
    length = prefix_len[group_id]
    positions = length + jnp.arange(stretch_rows, dtype=jnp.int32)
    cosine, sine = rope_tables(positions)

    slot_ids = jnp.arange(holder_cap, dtype=jnp.int32)
    holds_hit = hit_holder == group_id
    hit_order = jnp.cumsum(holds_hit.astype(jnp.int32), axis=1) - 1
    picked = holds_hit[:, None, :] & (hit_order[:, None, :] == slot_ids[None, :, None])
    sources = jnp.sum(jnp.where(picked, hit_slot[:, None, :], 0), axis=2)
    by_head = kv_pool.reshape(-1, block_rows, 2, KVH, HD)[sources]
    by_head = jnp.transpose(by_head, (0, 4, 1, 2, 3, 5))
    by_head = jnp.repeat(by_head, heads_share, axis=1)
    sending = by_head.reshape(
        request_count * cp_count, holder_cap * block_rows, 2 * HD
    )
    arrived = lax.all_to_all(sending, ("req", "cp"), split_axis=0, concat_axis=0, tiled=True)

    gathered = lax.all_gather(hidden[0], "cp", axis=0, tiled=True)
    raw_queries = jnp.dot(gathered, w_query, preferred_element_type=jnp.float32)
    columns = lax.dynamic_slice_in_dim(gathered, cp_rank * slice_rows, slice_rows, 1)
    partial_kv = jnp.dot(columns, w_keyval, preferred_element_type=jnp.float32)
    partial_kv = jnp.transpose(
        partial_kv.reshape(stretch_rows, 2, KVH, HD), (2, 0, 1, 3)
    ).reshape(KVH, stretch_rows, 2 * HD)
    partial_kv = jnp.repeat(partial_kv, heads_share, axis=0)
    summed = lax.psum_scatter(partial_kv, "cp", scatter_dimension=0, tiled=True)[0]
    keys = summed[:, :HD]
    keys = keys * cosine + jnp.roll(keys, HD // 2, axis=1) * sine
    fresh = jnp.concatenate([keys, summed[:, HD:]], axis=1).astype(jnp.bfloat16)

    my_holders = hit_holder[group_id]
    hit_index = jnp.arange(prefix_blocks, dtype=jnp.int32)
    earlier = (my_holders[:, None] == my_holders[None, :]) & (
        hit_index[:, None] > hit_index[None, :]
    )
    hit_rank = jnp.sum(earlier.astype(jnp.int32), axis=1)
    arrived = arrived.reshape(request_count, cp_count, holder_cap, block_rows, 2 * HD)
    prefix = arrived[my_holders, :, hit_rank].reshape(prefix_blocks * BLK, 2 * HD)

    attended = attention(length, raw_queries, cosine, sine, prefix, fresh)

    if cp_count == 8:
        wide = w_out.shape[1] // 2
        sums = [
            scatter_sum(
                jnp.dot(
                    attended, w_out[:, at : at + wide], preferred_element_type=jnp.float32
                ).astype(jnp.bfloat16),
                cp_rank,
            )
            for at in range(0, w_out.shape[1], wide)
        ]
        projected = jnp.concatenate(sums, axis=1)
    else:
        projected = lax.psum_scatter(
            jnp.dot(attended, w_out, preferred_element_type=jnp.float32).astype(jnp.bfloat16),
            "cp",
            scatter_dimension=0,
            tiled=True,
        ).astype(jnp.float32)
    layer_out = (residual[0].astype(jnp.float32) + projected).astype(jnp.bfloat16)[None]

    my_owners = owner[group_id]
    block_ids = jnp.arange(new_blocks, dtype=jnp.int32)
    before = (my_owners[:, None] == my_owners[None, :]) & (block_ids[:, None] > block_ids[None, :])
    owner_rank = jnp.sum(before.astype(jnp.int32), axis=1)
    targets = jnp.arange(request_count, dtype=jnp.int32)[:, None, None]
    cap_ids = jnp.arange(owner_cap, dtype=jnp.int32)[None, :, None]
    chosen = (my_owners[None, None, :] == targets) & (owner_rank[None, None, :] == cap_ids)
    block_pick = jnp.sum(jnp.where(chosen, block_ids[None, None, :], 0), axis=2)
    present = jnp.any(chosen, axis=2)
    blocks = fresh.reshape(new_blocks, cp_count, block_rows, 2 * HD)[block_pick]
    blocks = jnp.where(present[:, :, None, None, None], blocks, jnp.zeros((), jnp.bfloat16))
    blocks = jnp.transpose(blocks, (0, 2, 1, 3, 4)).reshape(
        request_count * cp_count, owner_cap * block_rows, 2 * HD
    )
    landed = lax.all_to_all(blocks, ("req", "cp"), split_axis=0, concat_axis=0, tiled=True)
    landed = landed.reshape(request_count, cp_count, owner_cap, block_rows, 2, HD)[:, ::heads_share]
    new_cache = jnp.transpose(landed, (0, 2, 3, 4, 1, 5)).reshape(
        1, request_count * owner_cap, block_rows, 2 * KVH * HD
    )
    return (layer_out, new_cache)


def solution(mesh):
    in_specs = (
        P("req", "cp", None),
        P("req", "cp", None),
        P(None, "cp"),
        P("cp", None),
        P("cp", None),
        P("req", "cp", None),
        P(),
        P(),
        P(),
        P(),
    )
    out_specs = (P("req", "cp", None), P("req", None, "cp", None))
    return jax.shard_map(local, mesh=mesh, in_specs=in_specs, out_specs=out_specs, check_vma=False)
```

```python
import functools
import math

import jax
import jax.numpy as jnp
from jax import lax
from jax.experimental import pallas as pl
from jax.experimental.pallas import tpu as pltpu
from jax.sharding import PartitionSpec as P

KVH = 8
HD = 128
BLK = 128
LOG2E = 1.4426950408889634


def frequencies(width):
    half_width = width // 2
    base_freq = jnp.power(
        jnp.float32(500000.0), -jnp.arange(half_width, dtype=jnp.float32) * (2.0 / width)
    )
    wavelength = 2.0 * math.pi / base_freq
    blended = (8192.0 / wavelength - 1.0) / 3.0
    middle = (1.0 - blended) * base_freq / 8.0 + blended * base_freq
    return jnp.where(
        wavelength < 2048.0, base_freq, jnp.where(wavelength > 8192.0, base_freq / 8.0, middle)
    )


def rope_tables(positions):
    angles = positions.astype(jnp.float32)[:, None] * frequencies(HD)[None, :]
    cosine, sine = jnp.cos(angles), jnp.sin(angles)
    return jnp.concatenate([cosine, cosine], axis=1), jnp.concatenate([-sine, sine], axis=1)


def pack_kernel(heads_share, group_ref, holder_ref, slot_ref, pool_ref, out_ref):
    key_width = KVH * HD
    for request in range(holder_ref.shape[0]):

        def one(index, count):
            mine = holder_ref[request, index] == group_ref[0]

            @pl.when(mine)
            def _():
                rows = pool_ref[slot_ref[request, index]]
                for dest in range(out_ref.shape[1]):
                    at = dest // heads_share * HD
                    out_ref[request, dest, count] = jnp.concatenate(
                        [rows[:, at : at + HD], rows[:, key_width + at : key_width + at + HD]],
                        axis=1,
                    )

            return count + mine.astype(jnp.int32)

        lax.fori_loop(0, holder_ref.shape[1], one, jnp.int32(0))


def pack(group, hit_holder, hit_slot, kv_pool, cp_count, holder_cap):
    requests = hit_holder.shape[0]
    block_rows = kv_pool.shape[1]
    shape = (requests, cp_count, holder_cap, block_rows, 2 * HD)
    return pl.pallas_call(
        functools.partial(pack_kernel, cp_count // KVH),
        grid_spec=pltpu.PrefetchScalarGridSpec(
            num_scalar_prefetch=3,
            grid=(1,),
            in_specs=[pl.BlockSpec(kv_pool.shape, lambda i, *_: (0, 0, 0))],
            out_specs=pl.BlockSpec(shape, lambda i, *_: (0, 0, 0, 0, 0)),
        ),
        out_shape=jax.ShapeDtypeStruct(shape, kv_pool.dtype),
        compiler_params=pltpu.CompilerParams(vmem_limit_bytes=24 * 1024 * 1024),
    )(group, hit_holder, hit_slot, kv_pool)


def attention_kernel(
    tile, ordered, length_ref, group_ref, holder_ref,
    q_ref, cos_ref, sin_ref, arrived_ref, fresh_ref, out_ref, prefix_ref,
):
    group = group_ref[0]
    span = prefix_ref.shape[0]
    _, ranks, _, block_rows, _ = arrived_ref.shape
    blocks = holder_ref.shape[1]
    row0 = pl.program_id(1) * tile

    @pl.when((pl.program_id(0) == 0) & (pl.program_id(1) == 0))
    def _():
        def place(index, counts):
            if ordered:
                holder, rank = 0, index
            else:
                holder = holder_ref[group, index]
                rank = sum(jnp.where(holder == h, counts[h], 0) for h in range(len(counts)))
            for r in range(ranks):
                at = pl.multiple_of(index * (ranks * block_rows), ranks * block_rows)
                prefix_ref[pl.ds(at + r * block_rows, block_rows), :] = arrived_ref[holder, r, rank]
            return tuple(
                n + (holder == h).astype(jnp.int32) if not ordered else n
                for h, n in enumerate(counts)
            )

        lax.fori_loop(0, blocks, place, (jnp.int32(0),) * holder_ref.shape[0])

    seen = lax.broadcasted_iota(jnp.int32, (1, span), 1) < length_ref[group]
    bias = jnp.where(seen, 0.0, -1e30)
    columns = lax.broadcasted_iota(jnp.int32, (tile, fresh_ref.shape[0]), 1)
    rows = lax.broadcasted_iota(jnp.int32, (tile, fresh_ref.shape[0]), 0) + row0
    causal = columns <= rows
    factor = HD ** (-0.5) * LOG2E

    def scores(query, keys):
        return lax.dot_general(
            query, keys, (((1,), (1,)), ((), ())), preferred_element_type=jnp.float32
        )

    for head in range(q_ref.shape[1] // HD):
        lanes = slice(head * HD, (head + 1) * HD)
        raw = q_ref[:, lanes]
        query = raw * cos_ref[...] + pltpu.roll(raw, HD // 2, 1) * sin_ref[...]
        query = (query * factor).astype(jnp.bfloat16)
        old = scores(query, prefix_ref[:, :HD]) + bias
        new = jnp.where(causal, scores(query, fresh_ref[:, :HD]), -1e30)
        peak = jnp.maximum(
            jnp.max(old, axis=1, keepdims=True), jnp.max(new, axis=1, keepdims=True)
        )
        old, new = jnp.exp2(old - peak), jnp.exp2(new - peak)
        total = jnp.sum(old, axis=1, keepdims=True) + jnp.sum(new, axis=1, keepdims=True)
        mixed = jnp.dot(
            old.astype(jnp.bfloat16), prefix_ref[:, HD:], preferred_element_type=jnp.float32
        ) + jnp.dot(
            new.astype(jnp.bfloat16), fresh_ref[:, HD:], preferred_element_type=jnp.float32
        )
        out_ref[:, lanes] = (mixed / total).astype(jnp.bfloat16)


def attention(prefix_len, group, hit_holder, raw_queries, cosine, sine, arrived, fresh, ordered):
    rows, width = raw_queries.shape
    tile = min(256, rows)
    span = hit_holder.shape[1] * BLK
    keys = span + rows
    return pl.pallas_call(
        functools.partial(attention_kernel, tile, ordered),
        grid_spec=pltpu.PrefetchScalarGridSpec(
            num_scalar_prefetch=3,
            grid=(width // (2 * HD), rows // tile),
            in_specs=[
                pl.BlockSpec((tile, 2 * HD), lambda h, t, *_: (t, h)),
                pl.BlockSpec((tile, HD), lambda h, t, *_: (t, 0)),
                pl.BlockSpec((tile, HD), lambda h, t, *_: (t, 0)),
                pl.BlockSpec(arrived.shape, lambda h, t, *_: (0, 0, 0, 0, 0)),
                pl.BlockSpec(fresh.shape, lambda h, t, *_: (0, 0)),
            ],
            out_specs=pl.BlockSpec((tile, 2 * HD), lambda h, t, *_: (t, h)),
            scratch_shapes=[pltpu.VMEM((span, 2 * HD), jnp.bfloat16)],
        ),
        out_shape=jax.ShapeDtypeStruct((rows, width), jnp.bfloat16),
        compiler_params=pltpu.CompilerParams(vmem_limit_bytes=40 * 1024 * 1024),
        cost_estimate=pl.CostEstimate(
            flops=4 * rows * width * keys,
            bytes_accessed=rows * width * 6,
            transcendentals=rows * width // HD * keys,
        ),
    )(prefix_len, group, hit_holder, raw_queries, cosine, sine, arrived, fresh)


def stacked(refs, last):
    whole, low, high = refs[:6], refs[6:8], refs[8:10]
    tail = [jnp.where(last, h[...], l[...]) for l, h in zip(low, high)]
    return jnp.concatenate([r[...] for r in whole] + tail, axis=0)


def keyval_kernel(rank_ref, *refs):
    parts, weight_ref, out_ref = refs[:10], refs[10], refs[11]
    rank = rank_ref[0]
    rows = parts[0].shape[0]
    tokens = stacked(parts, rank >= 4)
    key_width = KVH * HD
    for head in range(KVH):
        for half in range(2):
            at = half * key_width + head * HD
            product = jnp.dot(
                tokens, weight_ref[:, at : at + HD], preferred_element_type=jnp.float32
            )
            for b in range(8):
                to = pl.multiple_of((rank ^ b) * rows, rows)
                out_ref[head, pl.ds(to, rows), half * HD : (half + 1) * HD] = product[
                    b * rows : (b + 1) * rows
                ]


def query_kernel(rank_ref, *refs):
    parts, weight_ref, out_ref, total_ref = refs[:10], refs[10], refs[11], refs[12]
    step = pl.program_id(0)
    rank = rank_ref[0]
    rows = parts[0].shape[0]
    tokens = stacked(parts, step >= 4)

    @pl.when(step == 0)
    def _():
        total_ref[...] = jnp.zeros_like(total_ref)

    total_ref[...] += jnp.dot(tokens, weight_ref[...], preferred_element_type=jnp.float32)

    @pl.when(step == pl.num_programs(0) - 1)
    def _():
        for b in range(8):
            to = pl.multiple_of((rank ^ b) * rows, rows)
            out_ref[pl.ds(to, rows), :] = total_ref[b * rows : (b + 1) * rows]


def part_specs(rows, depth, block):
    whole = pl.BlockSpec((rows, depth), lambda i, r: (0, block(i, r)))
    low = pl.BlockSpec((rows, depth), lambda i, r: (0, jnp.minimum(block(i, r), 3)))
    high = pl.BlockSpec((rows, depth), lambda i, r: (0, jnp.maximum(block(i, r) - 4, 0)))
    return [whole] * 6 + [low] * 2 + [high] * 2


def keyval_project(rank, parts, w_keyval):
    rows = parts[0].shape[0]
    depth, width = w_keyval.shape
    shape = (KVH, 8 * rows, 2 * HD)
    return pl.pallas_call(
        keyval_kernel,
        grid_spec=pltpu.PrefetchScalarGridSpec(
            num_scalar_prefetch=1,
            grid=(1,),
            in_specs=part_specs(rows, depth, lambda i, r: r[0])
            + [pl.BlockSpec((depth, width), lambda i, r: (0, 0))],
            out_specs=pl.BlockSpec(shape, lambda i, r: (0, 0, 0)),
        ),
        out_shape=jax.ShapeDtypeStruct(shape, jnp.float32),
        compiler_params=pltpu.CompilerParams(vmem_limit_bytes=24 * 1024 * 1024),
        cost_estimate=pl.CostEstimate(
            flops=16 * rows * depth * width, bytes_accessed=2 * depth * width, transcendentals=0
        ),
    )(rank, *parts, w_keyval)


def query_project(rank, parts, w_query):
    rows, depth = parts[0].shape
    width = w_query.shape[1]
    block = depth // 8
    return pl.pallas_call(
        query_kernel,
        grid_spec=pltpu.PrefetchScalarGridSpec(
            num_scalar_prefetch=1,
            grid=(8,),
            in_specs=part_specs(rows, block, lambda i, r: i)
            + [pl.BlockSpec((block, width), lambda i, r: (i, 0))],
            out_specs=pl.BlockSpec((8 * rows, width), lambda i, r: (0, 0)),
            scratch_shapes=[pltpu.VMEM((8 * rows, width), jnp.float32)],
        ),
        out_shape=jax.ShapeDtypeStruct((8 * rows, width), jnp.float32),
        compiler_params=pltpu.CompilerParams(vmem_limit_bytes=24 * 1024 * 1024),
        cost_estimate=pl.CostEstimate(
            flops=16 * rows * depth * width, bytes_accessed=2 * depth * width, transcendentals=0
        ),
    )(rank, *parts, w_query)


def gather_parts(own):
    half = own.shape[1] // 2
    near_x, near_y, near_core = swap(own, 2, 8), swap(own, 4, 8), swap(own, 1, 8)
    left = swap(near_y[:, :half], 2, 8)
    right = swap(near_x[:, half:], 4, 8)
    return [
        own, near_core, near_x, swap(near_x, 1, 8), near_y, swap(near_y, 1, 8),
        left, swap(left, 1, 8), right, swap(right, 1, 8),
    ]


def swap(array, bit, count):
    return lax.ppermute(array, "cp", [(i, i ^ bit) for i in range(count)])


def pick(array, index, axis):
    return lax.dynamic_index_in_dim(array, index, axis, keepdims=False)


def add(one, two):
    return one.astype(jnp.float32) + two.astype(jnp.float32)


def scatter_sum(part, rank):
    rows, width = part.shape
    core, x, y = rank % 2, rank // 2 % 2, rank // 4
    view = part.reshape(2, 2, 2, rows // 8, width)
    got = swap(pick(view, 1 - core, 2), 1, 8)
    pair = add(pick(view, core, 2), got).astype(jnp.bfloat16)
    half = width // 2
    one, two = pair[..., :half], pair[..., half:]
    got_one = swap(pick(one, 1 - x, 1), 2, 8)
    got_two = swap(pick(two, 1 - y, 0), 4, 8)
    one = add(pick(one, x, 1), got_one)
    two = add(pick(two, y, 0), got_two)
    end_one = swap(pick(one, 1 - y, 0).astype(jnp.bfloat16), 4, 8)
    end_two = swap(pick(two, 1 - x, 0).astype(jnp.bfloat16), 2, 8)
    one = add(pick(one, y, 0), end_one)
    two = add(pick(two, x, 0), end_two)
    return jnp.concatenate([one, two], axis=1)


def local(
    hidden, residual, w_query, w_keyval, w_out, kv_pool, prefix_len, hit_holder, hit_slot, owner
):
    cp_count = lax.axis_size("cp")
    group_id = lax.axis_index("req")
    cp_rank = lax.axis_index("cp")
    tok_rows = hidden.shape[1]
    stretch_rows = tok_rows * cp_count
    slice_rows = w_keyval.shape[0]
    block_rows = kv_pool.shape[1]
    request_count = hit_holder.shape[0]
    prefix_blocks = hit_holder.shape[1]
    new_blocks = owner.shape[1]
    owner_cap = (new_blocks + 1) // 2
    holder_cap = prefix_blocks // 2
    heads_share = cp_count // KVH
    length = prefix_len[group_id]
    positions = length + jnp.arange(stretch_rows, dtype=jnp.int32)
    cosine, sine = rope_tables(positions)

    group = group_id.reshape(1)
    rank = cp_rank.reshape(1)
    tiled = block_rows % 16 == 0
    if tiled:
        sending = pack(group, hit_holder, hit_slot, kv_pool, cp_count, holder_cap)
    else:
        slot_ids = jnp.arange(holder_cap, dtype=jnp.int32)
        holds_hit = hit_holder == group_id
        hit_order = jnp.cumsum(holds_hit.astype(jnp.int32), axis=1) - 1
        picked = holds_hit[:, None, :] & (hit_order[:, None, :] == slot_ids[None, :, None])
        sources = jnp.sum(jnp.where(picked, hit_slot[:, None, :], 0), axis=2)
        by_head = kv_pool.reshape(-1, block_rows, 2, KVH, HD)[sources]
        by_head = jnp.transpose(by_head, (0, 4, 1, 2, 3, 5))
        sending = jnp.repeat(by_head, heads_share, axis=1)
    sending = sending.reshape(request_count * cp_count, holder_cap * block_rows, 2 * HD)
    arrived = lax.all_to_all(sending, ("req", "cp"), split_axis=0, concat_axis=0, tiled=True)
    arrived = arrived.reshape(request_count, cp_count, holder_cap, block_rows, 2 * HD)

    if cp_count == 8:
        parts = gather_parts(hidden[0])
        partial_kv = keyval_project(rank, parts, w_keyval)
        raw_queries = query_project(rank, parts, w_query)
    else:
        gathered = lax.all_gather(hidden[0], "cp", axis=0, tiled=True)
        raw_queries = jnp.dot(gathered, w_query, preferred_element_type=jnp.float32)
        columns = lax.dynamic_slice_in_dim(gathered, cp_rank * slice_rows, slice_rows, 1)
        partial_kv = jnp.dot(columns, w_keyval, preferred_element_type=jnp.float32)
        partial_kv = jnp.transpose(
            partial_kv.reshape(stretch_rows, 2, KVH, HD), (2, 0, 1, 3)
        ).reshape(KVH, stretch_rows, 2 * HD)
        partial_kv = jnp.repeat(partial_kv, heads_share, axis=0)
    summed = lax.psum_scatter(partial_kv, "cp", scatter_dimension=0, tiled=True)[0]
    keys = summed[:, :HD]
    keys = keys * cosine + jnp.roll(keys, HD // 2, axis=1) * sine
    fresh = jnp.concatenate([keys, summed[:, HD:]], axis=1).astype(jnp.bfloat16)

    if not tiled:
        my_holders = hit_holder[group_id]
        hit_index = jnp.arange(prefix_blocks, dtype=jnp.int32)
        earlier = (my_holders[:, None] == my_holders[None, :]) & (
            hit_index[:, None] > hit_index[None, :]
        )
        hit_rank = jnp.sum(earlier.astype(jnp.int32), axis=1)
        arrived = arrived[my_holders, :, hit_rank].reshape(1, 1, prefix_blocks, BLK, 2 * HD)

    attended = attention(
        prefix_len, group, hit_holder, raw_queries, cosine, sine, arrived, fresh, not tiled
    )

    if cp_count == 8:
        wide = w_out.shape[1] // 2
        sums = [
            scatter_sum(
                jnp.dot(
                    attended, w_out[:, at : at + wide], preferred_element_type=jnp.float32
                ).astype(jnp.bfloat16),
                cp_rank,
            )
            for at in range(0, w_out.shape[1], wide)
        ]
        projected = jnp.concatenate(sums, axis=1)
    else:
        projected = lax.psum_scatter(
            jnp.dot(attended, w_out, preferred_element_type=jnp.float32).astype(jnp.bfloat16),
            "cp",
            scatter_dimension=0,
            tiled=True,
        ).astype(jnp.float32)
    layer_out = (residual[0].astype(jnp.float32) + projected).astype(jnp.bfloat16)[None]

    my_owners = owner[group_id]
    block_ids = jnp.arange(new_blocks, dtype=jnp.int32)
    before = (my_owners[:, None] == my_owners[None, :]) & (block_ids[:, None] > block_ids[None, :])
    owner_rank = jnp.sum(before.astype(jnp.int32), axis=1)
    targets = jnp.arange(request_count, dtype=jnp.int32)[:, None, None]
    cap_ids = jnp.arange(owner_cap, dtype=jnp.int32)[None, :, None]
    chosen = (my_owners[None, None, :] == targets) & (owner_rank[None, None, :] == cap_ids)
    block_pick = jnp.sum(jnp.where(chosen, block_ids[None, None, :], 0), axis=2)
    present = jnp.any(chosen, axis=2)
    blocks = fresh.reshape(new_blocks, cp_count, block_rows, 2 * HD)[block_pick]
    blocks = jnp.where(present[:, :, None, None, None], blocks, jnp.zeros((), jnp.bfloat16))
    blocks = jnp.transpose(blocks, (0, 2, 1, 3, 4)).reshape(
        request_count * cp_count, owner_cap * block_rows, 2 * HD
    )
    landed = lax.all_to_all(blocks, ("req", "cp"), split_axis=0, concat_axis=0, tiled=True)
    landed = landed.reshape(request_count, cp_count, owner_cap, block_rows, 2, HD)[:, ::heads_share]
    new_cache = jnp.transpose(landed, (0, 2, 3, 4, 1, 5)).reshape(
        1, request_count * owner_cap, block_rows, 2 * KVH * HD
    )
    return (layer_out, new_cache)


def solution(mesh):
    in_specs = (
        P("req", "cp", None),
        P("req", "cp", None),
        P(None, "cp"),
        P("cp", None),
        P("cp", None),
        P("req", "cp", None),
        P(),
        P(),
        P(),
        P(),
    )
    out_specs = (P("req", "cp", None), P("req", None, "cp", None))
    return jax.shard_map(local, mesh=mesh, in_specs=in_specs, out_specs=out_specs, check_vma=False)
```

```python
import functools
import math

import jax
import jax.numpy as jnp
from jax import lax
from jax.experimental import pallas as pl
from jax.experimental.pallas import tpu as pltpu
from jax.sharding import PartitionSpec as P

KVH = 8
HD = 128
BLK = 128
LOG2E = 1.4426950408889634


def frequencies(width):
    half_width = width // 2
    base_freq = jnp.power(
        jnp.float32(500000.0), -jnp.arange(half_width, dtype=jnp.float32) * (2.0 / width)
    )
    wavelength = 2.0 * math.pi / base_freq
    blended = (8192.0 / wavelength - 1.0) / 3.0
    middle = (1.0 - blended) * base_freq / 8.0 + blended * base_freq
    return jnp.where(
        wavelength < 2048.0, base_freq, jnp.where(wavelength > 8192.0, base_freq / 8.0, middle)
    )


def rope_tables(positions):
    angles = positions.astype(jnp.float32)[:, None] * frequencies(HD)[None, :]
    cosine, sine = jnp.cos(angles), jnp.sin(angles)
    return jnp.concatenate([cosine, cosine], axis=1), jnp.concatenate([-sine, sine], axis=1)


def split_kernel(pool_ref, hidden_ref, out_ref):
    key_width = KVH * HD
    slots, block_rows, _ = pool_ref.shape
    width = out_ref.shape[3]

    def one(slot, carry):
        rows = pool_ref[slot]
        for head in range(KVH):
            at = head * HD
            out_ref[head, slot] = jnp.concatenate(
                [rows[:, at : at + HD], rows[:, key_width + at : key_width + at + HD]], axis=1
            )
        return carry

    lax.fori_loop(0, slots, one, 0)
    rows, features = hidden_ref.shape
    share = features // KVH
    for dest in range(KVH):
        for chunk in range(share // width):
            at = dest * share + chunk * width
            for r in range(rows // block_rows):
                out_ref[dest, slots + chunk * (rows // block_rows) + r] = hidden_ref[
                    r * block_rows : (r + 1) * block_rows, at : at + width
                ]


def split_heads(kv_pool, own):
    slots, block_rows, _ = kv_pool.shape
    extra = own.size // (KVH * block_rows * 2 * HD)
    shape = (KVH, slots + extra, block_rows, 2 * HD)
    return pl.pallas_call(
        split_kernel,
        grid=(1,),
        in_specs=[
            pl.BlockSpec(kv_pool.shape, lambda i: (0, 0, 0)),
            pl.BlockSpec(own.shape, lambda i: (0, 0)),
        ],
        out_specs=pl.BlockSpec(shape, lambda i: (0, 0, 0, 0)),
        out_shape=jax.ShapeDtypeStruct(shape, kv_pool.dtype),
        compiler_params=pltpu.CompilerParams(vmem_limit_bytes=16 * 1024 * 1024),
    )(kv_pool, own)


def pack_kernel(group_ref, holder_ref, slot_ref, pool_ref, *out_refs):
    ranks, _, block_rows, _ = pool_ref.shape
    group = group_ref[0]
    main_ref = out_refs[0]
    cap = main_ref.shape[1]
    for distance, more_ref in enumerate(out_refs[1:], start=1):
        request = group ^ distance

        def one(index, count, more_ref=more_ref, request=request):
            mine = holder_ref[request, index] == group
            slot = slot_ref[request, index]

            @pl.when(mine & (count < cap))
            def _():
                for r in range(ranks):
                    rows = slice(r * block_rows, (r + 1) * block_rows)
                    main_ref[request, count, rows, :] = pool_ref[r, slot]

            @pl.when(mine & (count >= cap))
            def _():
                for r in range(ranks):
                    rows = slice(r * block_rows, (r + 1) * block_rows)
                    more_ref[count - cap, rows, :] = pool_ref[r, slot]

            return count + mine.astype(jnp.int32)

        lax.fori_loop(0, holder_ref.shape[1], one, jnp.int32(0))


def pack(group, hit_holder, hit_slot, pool, cap, base):
    ranks, slots, block_rows, width = pool.shape
    block = (ranks * block_rows, width)
    shapes = [(hit_holder.shape[0], base, *block)] + [(cap - base, *block)] * 3
    return pl.pallas_call(
        pack_kernel,
        grid_spec=pltpu.PrefetchScalarGridSpec(
            num_scalar_prefetch=3,
            grid=(1,),
            in_specs=[pl.BlockSpec(pool.shape, lambda i, *_: (0, 0, 0, 0))],
            out_specs=[
                pl.BlockSpec(shape, lambda i, *_, n=len(shape): (0,) * n) for shape in shapes
            ],
        ),
        out_shape=[jax.ShapeDtypeStruct(shape, pool.dtype) for shape in shapes],
        compiler_params=pltpu.CompilerParams(vmem_limit_bytes=24 * 1024 * 1024),
    )(group, hit_holder, hit_slot, pool)


def place_pieces(group, length, holder_ref, slot_ref, refs, prefix_ref):
    pool_ref, main_ref, near_ref, two_ref, three_ref = refs
    ranks, _, block_rows, _ = pool_ref.shape
    rows = ranks * block_rows
    base = main_ref.shape[1]

    def one(index, counts):
        holder = holder_ref[group, index]
        distance = holder ^ group
        count = sum(jnp.where(distance == d, counts[d], 0) for d in range(4))
        at = pl.multiple_of(index * rows, rows)
        seen = index * rows < length

        @pl.when(jnp.logical_not(seen))
        def _():
            prefix_ref[pl.ds(at, rows), :] = jnp.zeros((rows, 2 * HD), jnp.bfloat16)

        @pl.when(seen & (distance == 0))
        def _():
            slot = slot_ref[group, index]
            for r in range(ranks):
                prefix_ref[pl.ds(at + r * block_rows, block_rows), :] = pool_ref[r, slot]

        low = count < base
        rest = count - base

        @pl.when(seen & (distance != 0) & low)
        def _():
            prefix_ref[pl.ds(at, rows), :] = main_ref[holder, count]

        def take(when, ref, n):
            @pl.when(seen & when)
            def _():
                prefix_ref[pl.ds(at, rows), :] = ref[n]

        take((distance == 1) & ~low, near_ref, rest)
        take((distance == 2) & ~low, two_ref, rest)
        take((distance == 3) & ~low, three_ref, rest)
        return tuple(n + (distance == d).astype(jnp.int32) for d, n in enumerate(counts))

    lax.fori_loop(0, holder_ref.shape[1], one, (jnp.int32(0),) * 4)


def attention_kernel(
    tile, ordered, length_ref, group_ref, holder_ref, slot_ref, q_ref, cos_ref, sin_ref, summed_ref, *refs
):
    *piece_refs, out_ref, fresh_ref, prefix_ref = refs
    group = group_ref[0]
    span = prefix_ref.shape[0]
    row0 = pl.program_id(1) * tile

    @pl.when((pl.program_id(0) == 0) & (pl.program_id(1) == 0))
    def _():
        if ordered:
            prefix_ref[...] = piece_refs[0][...]
        else:
            place_pieces(group, length_ref[group], holder_ref, slot_ref, piece_refs, prefix_ref)
        keys = summed_ref[:, :HD]
        keys = keys * cos_ref[...] + pltpu.roll(keys, HD // 2, 1) * sin_ref[...]
        fresh_ref[:, :HD] = keys.astype(jnp.bfloat16)
        fresh_ref[:, HD:] = summed_ref[:, HD:].astype(jnp.bfloat16)

    seen = lax.broadcasted_iota(jnp.int32, (1, span), 1) < length_ref[group]
    bias = jnp.where(seen, 0.0, -1e30)
    columns = lax.broadcasted_iota(jnp.int32, (tile, fresh_ref.shape[0]), 1)
    rows = lax.broadcasted_iota(jnp.int32, (tile, fresh_ref.shape[0]), 0) + row0
    causal = columns <= rows
    cosine = cos_ref[pl.ds(pl.multiple_of(row0, tile), tile), :]
    sine = sin_ref[pl.ds(pl.multiple_of(row0, tile), tile), :]
    factor = HD ** (-0.5) * LOG2E

    def scores(query, keys):
        return lax.dot_general(
            query, keys, (((1,), (1,)), ((), ())), preferred_element_type=jnp.float32
        )

    for head in range(q_ref.shape[1] // HD):
        lanes = slice(head * HD, (head + 1) * HD)
        raw = q_ref[:, lanes]
        query = raw * cosine + pltpu.roll(raw, HD // 2, 1) * sine
        query = (query * factor).astype(jnp.bfloat16)
        old = scores(query, prefix_ref[:, :HD]) + bias
        new = jnp.where(causal, scores(query, fresh_ref[:, :HD]), -1e30)
        peak = jnp.maximum(
            jnp.max(old, axis=1, keepdims=True), jnp.max(new, axis=1, keepdims=True)
        )
        old, new = jnp.exp2(old - peak), jnp.exp2(new - peak)
        total = jnp.sum(old, axis=1, keepdims=True) + jnp.sum(new, axis=1, keepdims=True)
        mixed = jnp.dot(
            old.astype(jnp.bfloat16), prefix_ref[:, HD:], preferred_element_type=jnp.float32
        ) + jnp.dot(
            new.astype(jnp.bfloat16), fresh_ref[:, HD:], preferred_element_type=jnp.float32
        )
        out_ref[:, lanes] = (mixed / total).astype(jnp.bfloat16)


def attention(
    prefix_len, group, hit_holder, hit_slot, raw_queries, cosine, sine, summed, pieces, ordered
):
    rows, width = raw_queries.shape
    tile = min(256, rows)
    span = hit_holder.shape[1] * BLK
    keys = span + rows

    def whole(array):
        return pl.BlockSpec(array.shape, lambda h, t, *_: (0,) * array.ndim)

    return pl.pallas_call(
        functools.partial(attention_kernel, tile, ordered),
        grid_spec=pltpu.PrefetchScalarGridSpec(
            num_scalar_prefetch=4,
            grid=(width // (2 * HD), rows // tile),
            in_specs=[
                pl.BlockSpec((tile, 2 * HD), lambda h, t, *_: (t, h)),
                whole(cosine),
                whole(sine),
                whole(summed),
            ]
            + [whole(piece) for piece in pieces],
            out_specs=[pl.BlockSpec((tile, 2 * HD), lambda h, t, *_: (t, h)), whole(summed)],
            scratch_shapes=[pltpu.VMEM((span, 2 * HD), jnp.bfloat16)],
        ),
        out_shape=[
            jax.ShapeDtypeStruct((rows, width), jnp.bfloat16),
            jax.ShapeDtypeStruct(summed.shape, jnp.bfloat16),
        ],
        compiler_params=pltpu.CompilerParams(vmem_limit_bytes=40 * 1024 * 1024),
        cost_estimate=pl.CostEstimate(
            flops=4 * rows * width * keys,
            bytes_accessed=rows * width * 6,
            transcendentals=rows * width // HD * keys,
        ),
    )(prefix_len, group, hit_holder, hit_slot, raw_queries, cosine, sine, summed, *pieces)


PAIRS = ((0, 2), (1, 3), (0, 3), (1, 2))


def pairs_wanted(prefix_len, hit_holder, base):
    requests, blocks = hit_holder.shape
    starts = jnp.arange(blocks, dtype=jnp.int32) * BLK
    seen = starts[None, :] < prefix_len[:, None]
    holders = jnp.arange(requests, dtype=jnp.int32)
    held = (hit_holder[:, None, :] == holders[None, :, None]) & seen[:, None, :]
    over = jnp.sum(held.astype(jnp.int32), axis=2) > base
    bits = [[0] * requests for _ in range(requests)]
    for n, (one, other) in enumerate(PAIRS):
        bits[one][other] = bits[other][one] = n + 1
    numbers = jnp.asarray(bits, jnp.int32)
    flags = [jnp.any(over & (numbers == n + 1)) for n in range(len(PAIRS))]
    return sum(flag.astype(jnp.int32) << n for n, flag in enumerate(flags))


def exchange_more(more, wanted):
    def branch(bits):
        def run(two, three):
            out = []
            for array, at in ((two, 0), (three, 2)):
                pairs = [PAIRS[n] for n in (at, at + 1) if bits >> n & 1]
                moves = [pair for one, other in pairs for pair in ((one, other), (other, one))]
                out.append(lax.ppermute(array, "req", moves) if moves else array)
            return tuple(out)

        return run

    return list(lax.switch(wanted, [branch(bits) for bits in range(16)], *more))


def keyval_kernel(slots, rows, mixed_ref, weight_ref, out_ref):
    ranks, groups, block_rows, width = mixed_ref.shape
    tall = rows // block_rows
    tokens = jnp.concatenate(
        [
            jnp.concatenate(
                [
                    mixed_ref[r, at + i]
                    for at in range(slots, groups, tall)
                ],
                axis=1,
            )
            for r in range(ranks)
            for i in range(tall)
        ],
        axis=0,
    )
    key_width = KVH * HD
    product = jnp.dot(tokens, weight_ref[...], preferred_element_type=jnp.float32)
    for head in range(KVH):
        at = head * HD
        out_ref[head, :, :HD] = product[:, at : at + HD]
        out_ref[head, :, HD:] = product[:, key_width + at : key_width + at + HD]


def keyval_project(mixed, slots, rows, w_keyval):
    depth, width = w_keyval.shape
    count = mixed.shape[0] * rows
    shape = (KVH, count, 2 * HD)
    return pl.pallas_call(
        functools.partial(keyval_kernel, slots, rows),
        grid=(1,),
        in_specs=[
            pl.BlockSpec(mixed.shape, lambda i: (0, 0, 0, 0)),
            pl.BlockSpec((depth, width), lambda i: (0, 0)),
        ],
        out_specs=pl.BlockSpec(shape, lambda i: (0, 0, 0)),
        out_shape=jax.ShapeDtypeStruct(shape, jnp.float32),
        compiler_params=pltpu.CompilerParams(vmem_limit_bytes=24 * 1024 * 1024),
        cost_estimate=pl.CostEstimate(flops=1024, bytes_accessed=1024, transcendentals=0),
    )(mixed, w_keyval)


def query_kernel(rank_ref, *refs):
    parts, weight_ref, out_ref, tokens_ref = refs[:10], refs[10], refs[11], refs[12]
    rank = rank_ref[0]
    rows, half = parts[6].shape

    @pl.when(pl.program_id(0) == 0)
    def _():
        for b in range(8):
            to = pl.multiple_of((rank ^ b) * rows, rows)
            if b < 6:
                tokens_ref[pl.ds(to, rows), :] = parts[b][...]
            else:
                tokens_ref[pl.ds(to, rows), :half] = parts[b][...]
                tokens_ref[pl.ds(to, rows), half:] = parts[b + 2][...]

    out_ref[...] = jnp.dot(tokens_ref[...], weight_ref[...], preferred_element_type=jnp.float32)


def query_project(rank, parts, w_query):
    rows, depth = parts[0].shape
    width = w_query.shape[1]
    block = 256
    return pl.pallas_call(
        query_kernel,
        grid_spec=pltpu.PrefetchScalarGridSpec(
            num_scalar_prefetch=1,
            grid=(width // block,),
            in_specs=[pl.BlockSpec(part.shape, lambda i, r: (0, 0)) for part in parts]
            + [pl.BlockSpec((depth, block), lambda i, r: (0, i))],
            out_specs=pl.BlockSpec((8 * rows, block), lambda i, r: (0, i)),
            scratch_shapes=[pltpu.VMEM((8 * rows, depth), jnp.bfloat16)],
        ),
        out_shape=jax.ShapeDtypeStruct((8 * rows, width), jnp.float32),
        compiler_params=pltpu.CompilerParams(vmem_limit_bytes=50 * 1024 * 1024),
        cost_estimate=pl.CostEstimate(flops=1024, bytes_accessed=1024, transcendentals=0),
    )(rank, *parts, w_query)


def gather_parts(own):
    half = own.shape[1] // 2
    near_x, near_y, near_core = swap(own, 2, 8), swap(own, 4, 8), swap(own, 1, 8)
    left = swap(near_y[:, :half], 2, 8)
    right = swap(near_x[:, half:], 4, 8)
    return [
        own, near_core, near_x, swap(near_x, 1, 8), near_y, swap(near_y, 1, 8),
        left, swap(left, 1, 8), right, swap(right, 1, 8),
    ]


def swap(array, bit, count):
    return lax.ppermute(array, "cp", [(i, i ^ bit) for i in range(count)])


def pick(array, index, axis):
    return lax.dynamic_index_in_dim(array, index, axis, keepdims=False)


def add(one, two):
    return one.astype(jnp.float32) + two.astype(jnp.float32)


def scatter_sum(part, rank):
    rows, width = part.shape
    core, x, y = rank % 2, rank // 2 % 2, rank // 4
    view = part.reshape(2, 2, 2, rows // 8, width)
    got = swap(pick(view, 1 - core, 2), 1, 8)
    pair = add(pick(view, core, 2), got).astype(jnp.bfloat16)
    half = width // 2
    one, two = pair[..., :half], pair[..., half:]
    got_one = swap(pick(one, 1 - x, 1), 2, 8)
    got_two = swap(pick(two, 1 - y, 0), 4, 8)
    one = add(pick(one, x, 1), got_one)
    two = add(pick(two, y, 0), got_two)
    end_one = swap(pick(one, 1 - y, 0).astype(jnp.bfloat16), 4, 8)
    end_two = swap(pick(two, 1 - x, 0).astype(jnp.bfloat16), 2, 8)
    one = add(pick(one, y, 0), end_one)
    two = add(pick(two, x, 0), end_two)
    return jnp.concatenate([one, two], axis=1)


def local(
    hidden, residual, w_query, w_keyval, w_out, kv_pool, prefix_len, hit_holder, hit_slot, owner
):
    cp_count = lax.axis_size("cp")
    group_id = lax.axis_index("req")
    cp_rank = lax.axis_index("cp")
    tok_rows = hidden.shape[1]
    stretch_rows = tok_rows * cp_count
    slice_rows = w_keyval.shape[0]
    block_rows = kv_pool.shape[1]
    request_count = hit_holder.shape[0]
    prefix_blocks = hit_holder.shape[1]
    new_blocks = owner.shape[1]
    owner_cap = (new_blocks + 1) // 2
    holder_cap = prefix_blocks // 2
    heads_share = cp_count // KVH
    length = prefix_len[group_id]
    positions = length + jnp.arange(stretch_rows, dtype=jnp.int32)
    cosine, sine = rope_tables(positions)

    group = group_id.reshape(1)
    rank = cp_rank.reshape(1)
    fast = cp_count == 8 and request_count == 4 and block_rows % 16 == 0
    own = hidden[0]
    if fast:
        pool = lax.all_to_all(
            split_heads(kv_pool, own), "cp", split_axis=0, concat_axis=0, tiled=True
        )
        base = holder_cap // 2
        wanted = pairs_wanted(prefix_len, hit_holder, base)
        pool, cosine, sine, wanted = lax.optimization_barrier((pool, cosine, sine, wanted))
        packed = pack(group, hit_holder, hit_slot, pool, holder_cap, base)
        own, pool, packed = lax.optimization_barrier((own, pool, packed))
        main, near, two_more, three_more = packed
        main = lax.all_to_all(main, "req", split_axis=0, concat_axis=0, tiled=True)
        near = lax.ppermute(near, "req", [(i, i ^ 1) for i in range(4)])
        partial_kv = keyval_project(pool, kv_pool.shape[0], tok_rows, w_keyval)
        summed = lax.psum_scatter(partial_kv, "cp", scatter_dimension=0, tiled=True)[0]
        raw_queries = query_project(rank, gather_parts(own), w_query)
        more, raw_queries = lax.optimization_barrier(((two_more, three_more), raw_queries))
        pieces = [pool, main, near] + exchange_more(more, wanted)
    else:
        slot_ids = jnp.arange(holder_cap, dtype=jnp.int32)
        holds_hit = hit_holder == group_id
        hit_order = jnp.cumsum(holds_hit.astype(jnp.int32), axis=1) - 1
        picked = holds_hit[:, None, :] & (hit_order[:, None, :] == slot_ids[None, :, None])
        sources = jnp.sum(jnp.where(picked, hit_slot[:, None, :], 0), axis=2)
        by_head = kv_pool.reshape(-1, block_rows, 2, KVH, HD)[sources]
        by_head = jnp.transpose(by_head, (0, 4, 1, 2, 3, 5))
        sending = jnp.repeat(by_head, heads_share, axis=1).reshape(
            request_count * cp_count, holder_cap * block_rows, 2 * HD
        )
        arrived = lax.all_to_all(sending, ("req", "cp"), split_axis=0, concat_axis=0, tiled=True)
        arrived = arrived.reshape(request_count, cp_count, holder_cap, block_rows, 2 * HD)
        my_holders = hit_holder[group_id]
        hit_index = jnp.arange(prefix_blocks, dtype=jnp.int32)
        earlier = (my_holders[:, None] == my_holders[None, :]) & (
            hit_index[:, None] > hit_index[None, :]
        )
        hit_rank = jnp.sum(earlier.astype(jnp.int32), axis=1)
        pieces = [arrived[my_holders, :, hit_rank].reshape(prefix_blocks * BLK, 2 * HD)]

        gathered = lax.all_gather(own, "cp", axis=0, tiled=True)
        raw_queries = jnp.dot(gathered, w_query, preferred_element_type=jnp.float32)
        columns = lax.dynamic_slice_in_dim(gathered, cp_rank * slice_rows, slice_rows, 1)
        partial_kv = jnp.dot(columns, w_keyval, preferred_element_type=jnp.float32)
        partial_kv = jnp.transpose(
            partial_kv.reshape(stretch_rows, 2, KVH, HD), (2, 0, 1, 3)
        ).reshape(KVH, stretch_rows, 2 * HD)
        partial_kv = jnp.repeat(partial_kv, heads_share, axis=0)
        summed = lax.psum_scatter(partial_kv, "cp", scatter_dimension=0, tiled=True)[0]
    attended, fresh = attention(
        prefix_len, group, hit_holder, hit_slot, raw_queries, cosine, sine, summed, pieces, not fast
    )

    if fast:
        wide = w_out.shape[1] // 2
        sums = [
            scatter_sum(
                jnp.dot(
                    attended, w_out[:, at : at + wide], preferred_element_type=jnp.float32
                ).astype(jnp.bfloat16),
                cp_rank,
            )
            for at in range(0, w_out.shape[1], wide)
        ]
        projected = jnp.concatenate(sums, axis=1)
    else:
        projected = lax.psum_scatter(
            jnp.dot(attended, w_out, preferred_element_type=jnp.float32).astype(jnp.bfloat16),
            "cp",
            scatter_dimension=0,
            tiled=True,
        ).astype(jnp.float32)
    layer_out = (residual[0].astype(jnp.float32) + projected).astype(jnp.bfloat16)[None]

    my_owners = owner[group_id]
    block_ids = jnp.arange(new_blocks, dtype=jnp.int32)
    before = (my_owners[:, None] == my_owners[None, :]) & (block_ids[:, None] > block_ids[None, :])
    owner_rank = jnp.sum(before.astype(jnp.int32), axis=1)
    targets = jnp.arange(request_count, dtype=jnp.int32)[:, None, None]
    cap_ids = jnp.arange(owner_cap, dtype=jnp.int32)[None, :, None]
    chosen = (my_owners[None, None, :] == targets) & (owner_rank[None, None, :] == cap_ids)
    block_pick = jnp.sum(jnp.where(chosen, block_ids[None, None, :], 0), axis=2)
    present = jnp.any(chosen, axis=2)
    blocks = fresh.reshape(new_blocks, cp_count, block_rows, 2 * HD)[block_pick]
    blocks = jnp.where(present[:, :, None, None, None], blocks, jnp.zeros((), jnp.bfloat16))
    blocks = jnp.transpose(blocks, (0, 2, 1, 3, 4)).reshape(
        request_count * cp_count, owner_cap * block_rows, 2 * HD
    )
    blocks, _ = lax.optimization_barrier((blocks, attended))
    landed = lax.all_to_all(blocks, ("req", "cp"), split_axis=0, concat_axis=0, tiled=True)
    landed = landed.reshape(request_count, cp_count, owner_cap, block_rows, 2, HD)[:, ::heads_share]
    new_cache = jnp.transpose(landed, (0, 2, 3, 4, 1, 5)).reshape(
        1, request_count * owner_cap, block_rows, 2 * KVH * HD
    )
    return (layer_out, new_cache)


def solution(mesh):
    in_specs = (
        P("req", "cp", None),
        P("req", "cp", None),
        P(None, "cp"),
        P("cp", None),
        P("cp", None),
        P("req", "cp", None),
        P(),
        P(),
        P(),
        P(),
    )
    out_specs = (P("req", "cp", None), P("req", None, "cp", None))
    return jax.shard_map(local, mesh=mesh, in_specs=in_specs, out_specs=out_specs, check_vma=False)
```

```python
import functools
import math

import jax
import jax.numpy as jnp
from jax import lax
from jax.experimental import pallas as pl
from jax.experimental.pallas import tpu as pltpu
from jax.sharding import PartitionSpec as P

KVH = 8
HD = 128
BLK = 128
LOG2E = 1.4426950408889634


def frequencies(width):
    half_width = width // 2
    base_freq = jnp.power(
        jnp.float32(500000.0), -jnp.arange(half_width, dtype=jnp.float32) * (2.0 / width)
    )
    wavelength = 2.0 * math.pi / base_freq
    blended = (8192.0 / wavelength - 1.0) / 3.0
    middle = (1.0 - blended) * base_freq / 8.0 + blended * base_freq
    return jnp.where(
        wavelength < 2048.0, base_freq, jnp.where(wavelength > 8192.0, base_freq / 8.0, middle)
    )


def rope_tables(positions):
    angles = positions.astype(jnp.float32)[:, None] * frequencies(HD)[None, :]
    cosine, sine = jnp.cos(angles), jnp.sin(angles)
    return jnp.concatenate([cosine, cosine], axis=1), jnp.concatenate([-sine, sine], axis=1)


def split_kernel(pool_ref, hidden_ref, out_ref):
    key_width = KVH * HD
    slots, block_rows, _ = pool_ref.shape
    width = out_ref.shape[3]

    def one(slot, carry):
        rows = pool_ref[slot]
        for head in range(KVH):
            at = head * HD
            out_ref[head, slot] = jnp.concatenate(
                [rows[:, at : at + HD], rows[:, key_width + at : key_width + at + HD]], axis=1
            )
        return carry

    lax.fori_loop(0, slots, one, 0)
    rows, features = hidden_ref.shape
    share = features // KVH
    for dest in range(KVH):
        for chunk in range(share // width):
            at = dest * share + chunk * width
            for r in range(rows // block_rows):
                out_ref[dest, slots + chunk * (rows // block_rows) + r] = hidden_ref[
                    r * block_rows : (r + 1) * block_rows, at : at + width
                ]


def split_heads(kv_pool, own):
    slots, block_rows, _ = kv_pool.shape
    extra = own.size // (KVH * block_rows * 2 * HD)
    shape = (KVH, slots + extra, block_rows, 2 * HD)
    return pl.pallas_call(
        split_kernel,
        grid=(1,),
        in_specs=[
            pl.BlockSpec(kv_pool.shape, lambda i: (0, 0, 0)),
            pl.BlockSpec(own.shape, lambda i: (0, 0)),
        ],
        out_specs=pl.BlockSpec(shape, lambda i: (0, 0, 0, 0)),
        out_shape=jax.ShapeDtypeStruct(shape, kv_pool.dtype),
        compiler_params=pltpu.CompilerParams(vmem_limit_bytes=52 * 1024 * 1024),
    )(kv_pool, own)


def pack_kernel(slots, group_ref, rank_ref, holder_ref, slot_ref, pool_ref, weight_ref, *out_refs):
    ranks, groups, block_rows, _ = pool_ref.shape
    group = group_ref[0]
    main_ref, near_ref, two_ref, three_ref, send_ref, keep_ref = out_refs
    cap = main_ref.shape[1]
    for distance, more_ref in enumerate((near_ref, two_ref, three_ref), start=1):
        request = group ^ distance

        def one(index, count, more_ref=more_ref, request=request):
            mine = holder_ref[request, index] == group
            slot = slot_ref[request, index]

            @pl.when(mine & (count < cap))
            def _():
                for r in range(ranks):
                    rows = slice(r * block_rows, (r + 1) * block_rows)
                    main_ref[request, count, rows, :] = pool_ref[r, slot]

            @pl.when(mine & (count >= cap))
            def _():
                for r in range(ranks):
                    rows = slice(r * block_rows, (r + 1) * block_rows)
                    more_ref[count - cap, rows, :] = pool_ref[r, slot]

            return count + mine.astype(jnp.int32)

        lax.fori_loop(0, holder_ref.shape[1], one, jnp.int32(0))

    tall = send_ref.shape[1] // ranks // block_rows
    tokens = jnp.concatenate(
        [
            jnp.concatenate([pool_ref[r, at + i] for at in range(slots, groups, tall)], axis=1)
            for r in range(ranks)
            for i in range(tall)
        ],
        axis=0,
    )
    key_width = KVH * HD
    for head in range(KVH):
        at = head * HD
        weight = jnp.concatenate(
            [weight_ref[:, at : at + HD], weight_ref[:, key_width + at : key_width + at + HD]],
            axis=1,
        )
        product = jnp.dot(tokens, weight, preferred_element_type=jnp.float32)
        product = product.astype(send_ref.dtype)
        distance = head ^ rank_ref[0]

        @pl.when(distance % 2 == 1)
        def _(product=product, distance=distance):
            send_ref[distance // 2] = product

        @pl.when(distance % 2 == 0)
        def _(product=product, distance=distance):
            keep_ref[distance // 2] = product


def pack(group, rank, hit_holder, hit_slot, mixed, w_keyval, slots, tokens, cap, base):
    ranks, _, block_rows, width = mixed.shape
    block = (ranks * block_rows, width)
    shapes = [(hit_holder.shape[0], base, *block)] + [(cap - base, *block)] * 3
    shapes += [(KVH // 2, tokens, width)] * 2
    return pl.pallas_call(
        functools.partial(pack_kernel, slots),
        grid_spec=pltpu.PrefetchScalarGridSpec(
            num_scalar_prefetch=4,
            grid=(1,),
            in_specs=[
                pl.BlockSpec(mixed.shape, lambda i, *_: (0, 0, 0, 0)),
                pl.BlockSpec(w_keyval.shape, lambda i, *_: (0, 0)),
            ],
            out_specs=[
                pl.BlockSpec(shape, lambda i, *_, n=len(shape): (0,) * n) for shape in shapes
            ],
        ),
        out_shape=[jax.ShapeDtypeStruct(shape, mixed.dtype) for shape in shapes],
        compiler_params=pltpu.CompilerParams(vmem_limit_bytes=28 * 1024 * 1024),
    )(group, rank, hit_holder, hit_slot, mixed, w_keyval)


def fresh_kernel(summed_ref, cos_ref, sin_ref, fresh_ref):
    keys = summed_ref[:, :HD]
    keys = keys * cos_ref[...] + pltpu.roll(keys, HD // 2, 1) * sin_ref[...]
    fresh_ref[:, :HD] = keys.astype(jnp.bfloat16)
    fresh_ref[:, HD:] = summed_ref[:, HD:].astype(jnp.bfloat16)


def finish_fresh(summed, cosine, sine):
    return pl.pallas_call(
        fresh_kernel, out_shape=jax.ShapeDtypeStruct(summed.shape, jnp.bfloat16)
    )(summed, cosine, sine)


def place_pieces(group, length, holder_ref, slot_ref, refs, prefix_ref):
    pool_ref, main_ref, near_ref, two_ref, three_ref = refs
    ranks, _, block_rows, _ = pool_ref.shape
    rows = ranks * block_rows
    base = main_ref.shape[1]

    def one(index, counts):
        holder = holder_ref[group, index]
        distance = holder ^ group
        count = sum(jnp.where(distance == d, counts[d], 0) for d in range(4))
        at = pl.multiple_of(index * rows, rows)
        seen = index * rows < length

        @pl.when(jnp.logical_not(seen))
        def _():
            prefix_ref[pl.ds(at, rows), :] = jnp.zeros((rows, 2 * HD), jnp.bfloat16)

        @pl.when(seen & (distance == 0))
        def _():
            slot = slot_ref[group, index]
            for r in range(ranks):
                prefix_ref[pl.ds(at + r * block_rows, block_rows), :] = pool_ref[r, slot]

        low = count < base
        rest = count - base

        @pl.when(seen & (distance != 0) & low)
        def _():
            prefix_ref[pl.ds(at, rows), :] = main_ref[holder, count]

        def take(when, ref, n):
            @pl.when(seen & when)
            def _():
                prefix_ref[pl.ds(at, rows), :] = ref[n]

        take((distance == 1) & ~low, near_ref, rest)
        take((distance == 2) & ~low, two_ref, rest)
        take((distance == 3) & ~low, three_ref, rest)
        return tuple(n + (distance == d).astype(jnp.int32) for d, n in enumerate(counts))

    lax.fori_loop(0, holder_ref.shape[1], one, (jnp.int32(0),) * 4)


def attention_kernel(
    tile, ordered, length_ref, group_ref, rank_ref, holder_ref, slot_ref, q_ref, cos_ref, sin_ref, fresh_ref, *refs
):
    if ordered:
        *piece_refs, out_ref, prefix_ref = refs
    else:
        *piece_refs, weight_ref, send0, send1, keep0, keep1 = refs[:-5]
        prefix_ref, out_ref, rows_ref, held_ref, arrived = refs[-5:]
        fetch = pltpu.make_async_copy(weight_ref, held_ref, arrived)

        @pl.when(pl.program_id(0) == 0)
        def _():
            fetch.start()

    group = group_ref[0]
    span = prefix_ref.shape[0]
    row0 = pl.program_id(1) * tile

    @pl.when((pl.program_id(0) == 0) & (pl.program_id(1) == 0))
    def _():
        if ordered:
            prefix_ref[...] = piece_refs[0][...]
        else:
            place_pieces(group, length_ref[group], holder_ref, slot_ref, piece_refs, prefix_ref)

    seen = lax.broadcasted_iota(jnp.int32, (1, span), 1) < length_ref[group]
    bias = jnp.where(seen, 0.0, -1e30)
    columns = lax.broadcasted_iota(jnp.int32, (tile, fresh_ref.shape[0]), 1)
    rows = lax.broadcasted_iota(jnp.int32, (tile, fresh_ref.shape[0]), 0) + row0
    causal = columns <= rows
    cosine = cos_ref[pl.ds(pl.multiple_of(row0, tile), tile), :]
    sine = sin_ref[pl.ds(pl.multiple_of(row0, tile), tile), :]
    factor = HD ** (-0.5) * LOG2E

    def scores(query, keys):
        return lax.dot_general(
            query, keys, (((1,), (1,)), ((), ())), preferred_element_type=jnp.float32
        )

    for head in range(q_ref.shape[1] // HD):
        lanes = slice(head * HD, (head + 1) * HD)
        raw = q_ref[:, lanes]
        query = raw * cosine + pltpu.roll(raw, HD // 2, 1) * sine
        query = (query * factor).astype(jnp.bfloat16)
        old = scores(query, prefix_ref[:, :HD]) + bias
        new = jnp.where(causal, scores(query, fresh_ref[:, :HD]), -1e30)
        peak = jnp.maximum(
            jnp.max(old, axis=1, keepdims=True), jnp.max(new, axis=1, keepdims=True)
        )
        old, new = jnp.exp2(old - peak), jnp.exp2(new - peak)
        total = jnp.sum(old, axis=1, keepdims=True) + jnp.sum(new, axis=1, keepdims=True)
        mixed = jnp.dot(
            old.astype(jnp.bfloat16), prefix_ref[:, HD:], preferred_element_type=jnp.float32
        ) + jnp.dot(
            new.astype(jnp.bfloat16), fresh_ref[:, HD:], preferred_element_type=jnp.float32
        )
        mixed = (mixed / total).astype(jnp.bfloat16)
        if ordered:
            out_ref[:, lanes] = mixed
        else:
            out_ref[pl.program_id(0) * (q_ref.shape[1] // HD) + head] = mixed

    if not ordered:

        @pl.when(pl.program_id(0) == pl.num_programs(0) - 1)
        def _():
            fetch.wait()
            project_kernel(rank_ref[0], out_ref, rows_ref, held_ref, (send0, send1, keep0, keep1))


def project_kernel(rank, heads_ref, rows_ref, weight_ref, out_refs):
    quads, rows, width = out_refs[0].shape
    for head in range(heads_ref.shape[0]):
        for n in range(2 * quads):
            source = rank ^ (n % quads * 2) ^ (1 - n // quads)
            at = pl.multiple_of(source * rows, rows)
            rows_ref[n * rows : (n + 1) * rows, head * HD : (head + 1) * HD] = heads_ref[
                head, pl.ds(at, rows), :
            ]
    block = 1024
    for half in range(2):

        def one(step, carry, half=half):
            at = pl.multiple_of(step * block, block)
            source = pl.multiple_of(half * width + at, block)
            product = jnp.dot(
                rows_ref[...],
                weight_ref[:, pl.ds(source, block)],
                preferred_element_type=jnp.float32,
            ).astype(jnp.bfloat16)
            for n in range(quads):
                out_refs[half][n, :, pl.ds(at, block)] = product[n * rows : (n + 1) * rows]
                out_refs[2 + half][n, :, pl.ds(at, block)] = product[
                    (quads + n) * rows : (quads + n + 1) * rows
                ]
            return carry

        lax.fori_loop(0, width // block, one, 0)


def attention(
    prefix_len, group, rank, hit_holder, hit_slot, raw_queries, cosine, sine, fresh, pieces, w_out
):
    rows, width = raw_queries.shape
    tile = min(256, rows)
    span = hit_holder.shape[1] * BLK
    keys = span + rows
    ordered = w_out is None
    fixed = [cosine, sine, fresh, *pieces]

    def whole(array):
        return pl.BlockSpec(
            array.shape, lambda h, t, *_: (0,) * len(array.shape), pipeline_mode=pl.Buffered(1)
        )

    scratch = [pltpu.VMEM((span, 2 * HD), jnp.bfloat16)]
    in_specs = [pl.BlockSpec((tile, 2 * HD), lambda h, t, *_: (t, h))]
    in_specs += [whole(array) for array in fixed]
    if ordered:
        outs = [jax.ShapeDtypeStruct((rows, width), jnp.bfloat16)]
        out_specs = [pl.BlockSpec((tile, 2 * HD), lambda h, t, *_: (t, h))]
    else:
        fixed.append(w_out)
        in_specs.append(pl.BlockSpec(memory_space=pl.ANY))
        part = (4, rows // 8, w_out.shape[1] // 2)
        outs = [jax.ShapeDtypeStruct(part, jnp.bfloat16)] * 4
        out_specs = [pl.BlockSpec(part, lambda h, t, *_: (0, 0, 0))] * 4
        scratch += [
            pltpu.VMEM((width // HD, rows, HD), jnp.bfloat16),
            pltpu.VMEM((rows, width), jnp.bfloat16),
            pltpu.VMEM(w_out.shape, jnp.bfloat16),
            pltpu.SemaphoreType.DMA,
        ]
    return pl.pallas_call(
        functools.partial(attention_kernel, tile, ordered),
        grid_spec=pltpu.PrefetchScalarGridSpec(
            num_scalar_prefetch=5,
            grid=(width // (2 * HD), rows // tile),
            in_specs=in_specs,
            out_specs=out_specs,
            scratch_shapes=scratch,
        ),
        out_shape=outs,
        compiler_params=pltpu.CompilerParams(vmem_limit_bytes=60 * 1024 * 1024),
        cost_estimate=pl.CostEstimate(
            flops=4 * rows * width * keys,
            bytes_accessed=rows * width * 6,
            transcendentals=rows * width // HD * keys,
        ),
    )(prefix_len, group, rank, hit_holder, hit_slot, raw_queries, *fixed)


PAIRS = ((0, 2), (1, 3), (0, 3), (1, 2))


def pairs_wanted(prefix_len, hit_holder, base):
    requests, blocks = hit_holder.shape
    starts = jnp.arange(blocks, dtype=jnp.int32) * BLK
    seen = starts[None, :] < prefix_len[:, None]
    holders = jnp.arange(requests, dtype=jnp.int32)
    held = (hit_holder[:, None, :] == holders[None, :, None]) & seen[:, None, :]
    over = jnp.sum(held.astype(jnp.int32), axis=2) > base
    bits = [[0] * requests for _ in range(requests)]
    for n, (one, other) in enumerate(PAIRS):
        bits[one][other] = bits[other][one] = n + 1
    numbers = jnp.asarray(bits, jnp.int32)
    flags = [jnp.any(over & (numbers == n + 1)) for n in range(len(PAIRS))]
    return sum(flag.astype(jnp.int32) << n for n, flag in enumerate(flags))


def exchange_more(more, wanted):
    def branch(bits):
        def run(two, three):
            out = []
            for array, at in ((two, 0), (three, 2)):
                pairs = [PAIRS[n] for n in (at, at + 1) if bits >> n & 1]
                moves = [pair for one, other in pairs for pair in ((one, other), (other, one))]
                out.append(lax.ppermute(array, "req", moves) if moves else array)
            return tuple(out)

        return run

    return list(lax.switch(wanted, [branch(bits) for bits in range(16)], *more))


def query_kernel(tokens_ref, weight_ref, out_ref):
    out_ref[...] = jnp.dot(tokens_ref[...], weight_ref[...], preferred_element_type=jnp.float32)


def query_project(tokens, w_query):
    rows, depth = tokens.shape
    width = w_query.shape[1]
    block = 256
    return pl.pallas_call(
        query_kernel,
        grid=(width // block,),
        in_specs=[
            pl.BlockSpec((rows, depth), lambda i: (0, 0)),
            pl.BlockSpec((depth, block), lambda i: (0, i)),
        ],
        out_specs=pl.BlockSpec((rows, block), lambda i: (0, i)),
        out_shape=jax.ShapeDtypeStruct((rows, width), jnp.float32),
        compiler_params=pltpu.CompilerParams(vmem_limit_bytes=50 * 1024 * 1024),
        cost_estimate=pl.CostEstimate(flops=1024, bytes_accessed=1024, transcendentals=0),
    )(tokens, w_query)


def swap(array, bit):
    return lax.ppermute(array, "cp", [(i, i ^ bit) for i in range(8)])


def add(one, two):
    return one.astype(jnp.float32) + two.astype(jnp.float32)


def halves(send, keep):
    got = swap(send, 1)
    half = keep.shape[2] // 2
    left = [add(keep[n::2, :, :half], got[n::2, :, :half]) for n in (0, 1)]
    right = [
        add(keep[2 * n : 2 * n + 2, :, half:], got[2 * n : 2 * n + 2, :, half:]) for n in (0, 1)
    ]
    return left[0], right[0], left[1].astype(send.dtype), right[1].astype(send.dtype)


def second_level(parts):
    left, right, to_x, to_y = parts
    return add(left, swap(to_x, 2)), add(right, swap(to_y, 4))


def third_level(parts, dtype):
    left, right = parts
    left = add(left[0], swap(left[1].astype(dtype), 4))
    right = add(right[0], swap(right[1].astype(dtype), 2))
    return jnp.concatenate([left, right], axis=1)


def local(
    hidden, residual, w_query, w_keyval, w_out, kv_pool, prefix_len, hit_holder, hit_slot, owner
):
    cp_count = lax.axis_size("cp")
    group_id = lax.axis_index("req")
    cp_rank = lax.axis_index("cp")
    tok_rows = hidden.shape[1]
    stretch_rows = tok_rows * cp_count
    slice_rows = w_keyval.shape[0]
    block_rows = kv_pool.shape[1]
    request_count = hit_holder.shape[0]
    prefix_blocks = hit_holder.shape[1]
    new_blocks = owner.shape[1]
    owner_cap = (new_blocks + 1) // 2
    holder_cap = prefix_blocks // 2
    heads_share = cp_count // KVH
    length = prefix_len[group_id]
    positions = length + jnp.arange(stretch_rows, dtype=jnp.int32)
    cosine, sine = rope_tables(positions)

    group = group_id.reshape(1)
    rank = cp_rank.reshape(1)
    fast = cp_count == 8 and request_count == 4 and block_rows % 16 == 0
    own = hidden[0]
    if fast:
        pool = lax.all_to_all(
            split_heads(kv_pool, own), "cp", split_axis=0, concat_axis=0, tiled=True
        )
        base = holder_cap // 2
        wanted = pairs_wanted(prefix_len, hit_holder, base)
        own, pool, cosine, sine, wanted = lax.optimization_barrier(
            (own, pool, cosine, sine, wanted)
        )
        packed = pack(
            group, rank, hit_holder, hit_slot, pool, w_keyval,
            kv_pool.shape[0], stretch_rows, holder_cap, base,
        )
        main, near, two_more, three_more, *terms = packed
        main = lax.all_to_all(main, "req", split_axis=0, concat_axis=0, tiled=True)
        near = lax.ppermute(near, "req", [(i, i ^ 1) for i in range(4)])
        summed = third_level(second_level(halves(*terms)), terms[0].dtype)
        fresh = finish_fresh(summed, cosine, sine)
        gathered = lax.all_gather(own, "cp", axis=0, tiled=True)
        raw_queries = query_project(gathered, w_query)
        pieces = [pool, main, near] + exchange_more((two_more, three_more), wanted)
    else:
        slot_ids = jnp.arange(holder_cap, dtype=jnp.int32)
        holds_hit = hit_holder == group_id
        hit_order = jnp.cumsum(holds_hit.astype(jnp.int32), axis=1) - 1
        picked = holds_hit[:, None, :] & (hit_order[:, None, :] == slot_ids[None, :, None])
        sources = jnp.sum(jnp.where(picked, hit_slot[:, None, :], 0), axis=2)
        by_head = kv_pool.reshape(-1, block_rows, 2, KVH, HD)[sources]
        by_head = jnp.transpose(by_head, (0, 4, 1, 2, 3, 5))
        sending = jnp.repeat(by_head, heads_share, axis=1).reshape(
            request_count * cp_count, holder_cap * block_rows, 2 * HD
        )
        arrived = lax.all_to_all(sending, ("req", "cp"), split_axis=0, concat_axis=0, tiled=True)
        arrived = arrived.reshape(request_count, cp_count, holder_cap, block_rows, 2 * HD)
        my_holders = hit_holder[group_id]
        hit_index = jnp.arange(prefix_blocks, dtype=jnp.int32)
        earlier = (my_holders[:, None] == my_holders[None, :]) & (
            hit_index[:, None] > hit_index[None, :]
        )
        hit_rank = jnp.sum(earlier.astype(jnp.int32), axis=1)
        pieces = [arrived[my_holders, :, hit_rank].reshape(prefix_blocks * BLK, 2 * HD)]

        gathered = lax.all_gather(own, "cp", axis=0, tiled=True)
        raw_queries = jnp.dot(gathered, w_query, preferred_element_type=jnp.float32)
        columns = lax.dynamic_slice_in_dim(gathered, cp_rank * slice_rows, slice_rows, 1)
        partial_kv = jnp.dot(columns, w_keyval, preferred_element_type=jnp.float32)
        partial_kv = jnp.transpose(
            partial_kv.reshape(stretch_rows, 2, KVH, HD), (2, 0, 1, 3)
        ).reshape(KVH, stretch_rows, 2 * HD)
        partial_kv = jnp.repeat(partial_kv, heads_share, axis=0)
        summed = lax.psum_scatter(partial_kv, "cp", scatter_dimension=0, tiled=True)[0]
        keys = summed[:, :HD]
        keys = keys * cosine + jnp.roll(keys, HD // 2, axis=1) * sine
        fresh = jnp.concatenate([keys, summed[:, HD:]], axis=1).astype(jnp.bfloat16)
    outs = attention(
        prefix_len, group, rank, hit_holder, hit_slot, raw_queries, cosine, sine, fresh, pieces,
        w_out if fast else None,
    )
    my_owners = owner[group_id]
    block_ids = jnp.arange(new_blocks, dtype=jnp.int32)
    before = (my_owners[:, None] == my_owners[None, :]) & (block_ids[:, None] > block_ids[None, :])
    owner_rank = jnp.sum(before.astype(jnp.int32), axis=1)
    targets = jnp.arange(request_count, dtype=jnp.int32)[:, None, None]
    cap_ids = jnp.arange(owner_cap, dtype=jnp.int32)[None, :, None]
    chosen = (my_owners[None, None, :] == targets) & (owner_rank[None, None, :] == cap_ids)
    block_pick = jnp.sum(jnp.where(chosen, block_ids[None, None, :], 0), axis=2)
    present = jnp.any(chosen, axis=2)
    blocks = fresh.reshape(new_blocks, cp_count, block_rows, 2 * HD)[block_pick]
    blocks = jnp.where(present[:, :, None, None, None], blocks, jnp.zeros((), jnp.bfloat16))
    blocks = jnp.transpose(blocks, (0, 2, 1, 3, 4)).reshape(
        request_count * cp_count, owner_cap * block_rows, 2 * HD
    )

    if fast:
        send0, send1, keep0, keep1 = outs
        terms = [halves(send0, keep0), halves(send1, keep1)]
        blocks, terms[1] = lax.optimization_barrier((blocks, terms[1]))
        terms = [second_level(term) for term in terms]
        projected = jnp.concatenate([third_level(term, jnp.bfloat16) for term in terms], axis=1)
    else:
        (attended,) = outs
        projected = lax.psum_scatter(
            jnp.dot(attended, w_out, preferred_element_type=jnp.float32).astype(jnp.bfloat16),
            "cp",
            scatter_dimension=0,
            tiled=True,
        ).astype(jnp.float32)
    layer_out = (residual[0].astype(jnp.float32) + projected).astype(jnp.bfloat16)[None]

    landed = lax.all_to_all(blocks, ("req", "cp"), split_axis=0, concat_axis=0, tiled=True)
    landed = landed.reshape(request_count, cp_count, owner_cap, block_rows, 2, HD)[:, ::heads_share]
    new_cache = jnp.transpose(landed, (0, 2, 3, 4, 1, 5)).reshape(
        1, request_count * owner_cap, block_rows, 2 * KVH * HD
    )
    return (layer_out, new_cache)


def solution(mesh):
    in_specs = (
        P("req", "cp", None),
        P("req", "cp", None),
        P(None, "cp"),
        P("cp", None),
        P("cp", None),
        P("req", "cp", None),
        P(),
        P(),
        P(),
        P(),
    )
    out_specs = (P("req", "cp", None), P("req", None, "cp", None))
    return jax.shard_map(local, mesh=mesh, in_specs=in_specs, out_specs=out_specs, check_vma=False)
```

```python
import functools
import math

import jax
import jax.numpy as jnp
from jax import lax
from jax.experimental import pallas as pl
from jax.experimental.pallas import tpu as pltpu
from jax.sharding import PartitionSpec as P

KVH = 8
HD = 128
BLK = 128
LOG2E = 1.4426950408889634


def frequencies(width):
    half_width = width // 2
    base_freq = jnp.power(
        jnp.float32(500000.0), -jnp.arange(half_width, dtype=jnp.float32) * (2.0 / width)
    )
    wavelength = 2.0 * math.pi / base_freq
    blended = (8192.0 / wavelength - 1.0) / 3.0
    middle = (1.0 - blended) * base_freq / 8.0 + blended * base_freq
    return jnp.where(
        wavelength < 2048.0, base_freq, jnp.where(wavelength > 8192.0, base_freq / 8.0, middle)
    )


def rope_tables(positions):
    angles = positions.astype(jnp.float32)[:, None] * frequencies(HD)[None, :]
    cosine, sine = jnp.cos(angles), jnp.sin(angles)
    return jnp.concatenate([cosine, cosine], axis=1), jnp.concatenate([-sine, sine], axis=1)


def split_kernel(pool_ref, hidden_ref, out_ref):
    key_width = KVH * HD
    slots, block_rows, _ = pool_ref.shape
    width = out_ref.shape[3]

    def one(slot, carry):
        rows = pool_ref[slot]
        for head in range(KVH):
            at = head * HD
            out_ref[head, slot] = jnp.concatenate(
                [rows[:, at : at + HD], rows[:, key_width + at : key_width + at + HD]], axis=1
            )
        return carry

    lax.fori_loop(0, slots, one, 0)
    rows, features = hidden_ref.shape
    share = features // KVH
    for dest in range(KVH):
        for chunk in range(share // width):
            at = dest * share + chunk * width
            for r in range(rows // block_rows):
                out_ref[dest, slots + chunk * (rows // block_rows) + r] = hidden_ref[
                    r * block_rows : (r + 1) * block_rows, at : at + width
                ]


def split_heads(kv_pool, own):
    slots, block_rows, _ = kv_pool.shape
    extra = own.size // (KVH * block_rows * 2 * HD)
    shape = (KVH, slots + extra, block_rows, 2 * HD)
    return pl.pallas_call(
        split_kernel,
        grid=(1,),
        in_specs=[
            pl.BlockSpec(kv_pool.shape, lambda i: (0, 0, 0)),
            pl.BlockSpec(own.shape, lambda i: (0, 0)),
        ],
        out_specs=pl.BlockSpec(shape, lambda i: (0, 0, 0, 0)),
        out_shape=jax.ShapeDtypeStruct(shape, kv_pool.dtype),
        compiler_params=pltpu.CompilerParams(vmem_limit_bytes=52 * 1024 * 1024),
    )(kv_pool, own)


def pack_kernel(slots, group_ref, rank_ref, holder_ref, slot_ref, pool_ref, weight_ref, *out_refs):
    ranks, groups, block_rows, _ = pool_ref.shape
    group = group_ref[0]
    main_ref, near_ref, two_ref, three_ref, send_ref, keep_ref = out_refs
    cap = main_ref.shape[1]
    for distance, more_ref in enumerate((near_ref, two_ref, three_ref), start=1):
        request = group ^ distance

        def one(index, count, more_ref=more_ref, request=request):
            mine = holder_ref[request, index] == group
            slot = slot_ref[request, index]

            @pl.when(mine & (count < cap))
            def _():
                for r in range(ranks):
                    rows = slice(r * block_rows, (r + 1) * block_rows)
                    main_ref[request, count, rows, :] = pool_ref[r, slot]

            @pl.when(mine & (count >= cap))
            def _():
                for r in range(ranks):
                    rows = slice(r * block_rows, (r + 1) * block_rows)
                    more_ref[count - cap, rows, :] = pool_ref[r, slot]

            return count + mine.astype(jnp.int32)

        lax.fori_loop(0, holder_ref.shape[1], one, jnp.int32(0))

    tall = send_ref.shape[1] // ranks // block_rows
    tokens = jnp.concatenate(
        [
            jnp.concatenate([pool_ref[r, at + i] for at in range(slots, groups, tall)], axis=1)
            for r in range(ranks)
            for i in range(tall)
        ],
        axis=0,
    )
    key_width = KVH * HD
    for head in range(KVH):
        at = head * HD
        weight = jnp.concatenate(
            [weight_ref[:, at : at + HD], weight_ref[:, key_width + at : key_width + at + HD]],
            axis=1,
        )
        product = jnp.dot(tokens, weight, preferred_element_type=jnp.float32)
        product = product.astype(send_ref.dtype)
        distance = head ^ rank_ref[0]

        @pl.when(distance % 2 == 1)
        def _(product=product, distance=distance):
            send_ref[distance // 2] = product

        @pl.when(distance % 2 == 0)
        def _(product=product, distance=distance):
            keep_ref[distance // 2] = product


def pack(group, rank, hit_holder, hit_slot, mixed, w_keyval, slots, tokens, cap, base):
    ranks, _, block_rows, width = mixed.shape
    block = (ranks * block_rows, width)
    shapes = [(hit_holder.shape[0], base, *block)] + [(cap - base, *block)] * 3
    shapes += [(KVH // 2, tokens, width)] * 2
    return pl.pallas_call(
        functools.partial(pack_kernel, slots),
        grid_spec=pltpu.PrefetchScalarGridSpec(
            num_scalar_prefetch=4,
            grid=(1,),
            in_specs=[
                pl.BlockSpec(mixed.shape, lambda i, *_: (0, 0, 0, 0)),
                pl.BlockSpec(w_keyval.shape, lambda i, *_: (0, 0)),
            ],
            out_specs=[
                pl.BlockSpec(shape, lambda i, *_, n=len(shape): (0,) * n) for shape in shapes
            ],
        ),
        out_shape=[jax.ShapeDtypeStruct(shape, mixed.dtype) for shape in shapes],
        compiler_params=pltpu.CompilerParams(vmem_limit_bytes=28 * 1024 * 1024),
    )(group, rank, hit_holder, hit_slot, mixed, w_keyval)


def fresh_kernel(summed_ref, cos_ref, sin_ref, fresh_ref):
    keys = summed_ref[:, :HD]
    keys = keys * cos_ref[...] + pltpu.roll(keys, HD // 2, 1) * sin_ref[...]
    fresh_ref[:, :HD] = keys.astype(jnp.bfloat16)
    fresh_ref[:, HD:] = summed_ref[:, HD:].astype(jnp.bfloat16)


def finish_fresh(summed, cosine, sine):
    return pl.pallas_call(
        fresh_kernel, out_shape=jax.ShapeDtypeStruct(summed.shape, jnp.bfloat16)
    )(summed, cosine, sine)


def place_pieces(group, length, holder_ref, slot_ref, refs, prefix_ref):
    pool_ref, main_ref, near_ref, two_ref, three_ref = refs
    ranks, _, block_rows, _ = pool_ref.shape
    rows = ranks * block_rows
    base = main_ref.shape[1]

    def one(index, counts):
        holder = holder_ref[group, index]
        distance = holder ^ group
        count = sum(jnp.where(distance == d, counts[d], 0) for d in range(4))
        at = pl.multiple_of(index * rows, rows)
        seen = index * rows < length

        @pl.when(jnp.logical_not(seen))
        def _():
            prefix_ref[pl.ds(at, rows), :] = jnp.zeros((rows, 2 * HD), jnp.bfloat16)

        @pl.when(seen & (distance == 0))
        def _():
            slot = slot_ref[group, index]
            for r in range(ranks):
                prefix_ref[pl.ds(at + r * block_rows, block_rows), :] = pool_ref[r, slot]

        low = count < base
        rest = count - base

        @pl.when(seen & (distance != 0) & low)
        def _():
            prefix_ref[pl.ds(at, rows), :] = main_ref[holder, count]

        def take(when, ref, n):
            @pl.when(seen & when)
            def _():
                prefix_ref[pl.ds(at, rows), :] = ref[n]

        take((distance == 1) & ~low, near_ref, rest)
        take((distance == 2) & ~low, two_ref, rest)
        take((distance == 3) & ~low, three_ref, rest)
        return tuple(n + (distance == d).astype(jnp.int32) for d, n in enumerate(counts))

    lax.fori_loop(0, holder_ref.shape[1], one, (jnp.int32(0),) * 4)


def attention_kernel(
    tile, ordered, length_ref, group_ref, rank_ref, holder_ref, slot_ref, q_ref, cos_ref, sin_ref, fresh_ref, *refs
):
    if ordered:
        *piece_refs, out_ref, prefix_ref = refs
    else:
        *piece_refs, weight_ref, send0, send1, keep0, keep1 = refs[:-5]
        prefix_ref, out_ref, rows_ref, held_ref, arrived = refs[-5:]
        fetch = pltpu.make_async_copy(weight_ref, held_ref, arrived)

        @pl.when(pl.program_id(0) == 0)
        def _():
            fetch.start()

    group = group_ref[0]
    span = prefix_ref.shape[0]
    row0 = pl.program_id(1) * tile

    @pl.when((pl.program_id(0) == 0) & (pl.program_id(1) == 0))
    def _():
        if ordered:
            prefix_ref[...] = piece_refs[0][...]
        else:
            place_pieces(group, length_ref[group], holder_ref, slot_ref, piece_refs, prefix_ref)

    seen = lax.broadcasted_iota(jnp.int32, (1, span), 1) < length_ref[group]
    bias = jnp.where(seen, 0.0, -1e30)
    columns = lax.broadcasted_iota(jnp.int32, (tile, fresh_ref.shape[0]), 1)
    rows = lax.broadcasted_iota(jnp.int32, (tile, fresh_ref.shape[0]), 0) + row0
    causal = columns <= rows
    cosine = cos_ref[pl.ds(pl.multiple_of(row0, tile), tile), :]
    sine = sin_ref[pl.ds(pl.multiple_of(row0, tile), tile), :]
    factor = HD ** (-0.5) * LOG2E

    def scores(query, keys):
        return lax.dot_general(
            query, keys, (((1,), (1,)), ((), ())), preferred_element_type=jnp.float32
        )

    for head in range(q_ref.shape[1] // HD):
        lanes = slice(head * HD, (head + 1) * HD)
        raw = q_ref[:, lanes]
        query = raw * cosine + pltpu.roll(raw, HD // 2, 1) * sine
        query = (query * factor).astype(jnp.bfloat16)
        old = scores(query, prefix_ref[:, :HD]) + bias
        new = jnp.where(causal, scores(query, fresh_ref[:, :HD]), -1e30)
        peak = jnp.maximum(
            jnp.max(old, axis=1, keepdims=True), jnp.max(new, axis=1, keepdims=True)
        )
        old, new = jnp.exp2(old - peak), jnp.exp2(new - peak)
        total = jnp.sum(old, axis=1, keepdims=True) + jnp.sum(new, axis=1, keepdims=True)
        mixed = jnp.dot(
            old.astype(jnp.bfloat16), prefix_ref[:, HD:], preferred_element_type=jnp.float32
        ) + jnp.dot(
            new.astype(jnp.bfloat16), fresh_ref[:, HD:], preferred_element_type=jnp.float32
        )
        mixed = (mixed / total).astype(jnp.bfloat16)
        if ordered:
            out_ref[:, lanes] = mixed
        else:
            out_ref[pl.program_id(0) * (q_ref.shape[1] // HD) + head] = mixed

    if not ordered:

        @pl.when(pl.program_id(0) == pl.num_programs(0) - 1)
        def _():
            fetch.wait()
            project_kernel(rank_ref[0], out_ref, rows_ref, held_ref, (send0, send1, keep0, keep1))


def project_kernel(rank, heads_ref, rows_ref, weight_ref, out_refs):
    quads, rows, width = out_refs[0].shape
    for head in range(heads_ref.shape[0]):
        for n in range(2 * quads):
            source = rank ^ (n % quads * 2) ^ (1 - n // quads)
            at = pl.multiple_of(source * rows, rows)
            rows_ref[n * rows : (n + 1) * rows, head * HD : (head + 1) * HD] = heads_ref[
                head, pl.ds(at, rows), :
            ]
    block = 1024
    for half in range(2):

        def one(step, carry, half=half):
            at = pl.multiple_of(step * block, block)
            source = pl.multiple_of(half * width + at, block)
            product = jnp.dot(
                rows_ref[...],
                weight_ref[:, pl.ds(source, block)],
                preferred_element_type=jnp.float32,
            ).astype(jnp.bfloat16)
            for n in range(quads):
                out_refs[half][n, :, pl.ds(at, block)] = product[n * rows : (n + 1) * rows]
                out_refs[2 + half][n, :, pl.ds(at, block)] = product[
                    (quads + n) * rows : (quads + n + 1) * rows
                ]
            return carry

        lax.fori_loop(0, width // block, one, 0)


def attention(
    prefix_len, group, rank, hit_holder, hit_slot, raw_queries, cosine, sine, fresh, pieces, w_out
):
    rows, width = raw_queries.shape
    tile = min(256, rows)
    span = hit_holder.shape[1] * BLK
    keys = span + rows
    ordered = w_out is None
    fixed = [cosine, sine, fresh, *pieces]

    def whole(array):
        return pl.BlockSpec(
            array.shape, lambda h, t, *_: (0,) * len(array.shape), pipeline_mode=pl.Buffered(1)
        )

    scratch = [pltpu.VMEM((span, 2 * HD), jnp.bfloat16)]
    in_specs = [pl.BlockSpec((tile, 2 * HD), lambda h, t, *_: (t, h))]
    in_specs += [whole(array) for array in fixed]
    if ordered:
        outs = [jax.ShapeDtypeStruct((rows, width), jnp.bfloat16)]
        out_specs = [pl.BlockSpec((tile, 2 * HD), lambda h, t, *_: (t, h))]
    else:
        fixed.append(w_out)
        in_specs.append(pl.BlockSpec(memory_space=pl.ANY))
        part = (4, rows // 8, w_out.shape[1] // 2)
        outs = [jax.ShapeDtypeStruct(part, jnp.bfloat16)] * 4
        out_specs = [pl.BlockSpec(part, lambda h, t, *_: (0, 0, 0))] * 4
        scratch += [
            pltpu.VMEM((width // HD, rows, HD), jnp.bfloat16),
            pltpu.VMEM((rows, width), jnp.bfloat16),
            pltpu.VMEM(w_out.shape, jnp.bfloat16),
            pltpu.SemaphoreType.DMA,
        ]
    return pl.pallas_call(
        functools.partial(attention_kernel, tile, ordered),
        grid_spec=pltpu.PrefetchScalarGridSpec(
            num_scalar_prefetch=5,
            grid=(width // (2 * HD), rows // tile),
            in_specs=in_specs,
            out_specs=out_specs,
            scratch_shapes=scratch,
        ),
        out_shape=outs,
        compiler_params=pltpu.CompilerParams(vmem_limit_bytes=60 * 1024 * 1024),
        cost_estimate=pl.CostEstimate(
            flops=4 * rows * width * keys,
            bytes_accessed=rows * width * 6,
            transcendentals=rows * width // HD * keys,
        ),
    )(prefix_len, group, rank, hit_holder, hit_slot, raw_queries, *fixed)


PAIRS = ((0, 2), (1, 3), (0, 3), (1, 2))


def pairs_wanted(prefix_len, hit_holder, base):
    requests, blocks = hit_holder.shape
    starts = jnp.arange(blocks, dtype=jnp.int32) * BLK
    seen = starts[None, :] < prefix_len[:, None]
    holders = jnp.arange(requests, dtype=jnp.int32)
    held = (hit_holder[:, None, :] == holders[None, :, None]) & seen[:, None, :]
    over = jnp.sum(held.astype(jnp.int32), axis=2) > base
    bits = [[0] * requests for _ in range(requests)]
    for n, (one, other) in enumerate(PAIRS):
        bits[one][other] = bits[other][one] = n + 1
    numbers = jnp.asarray(bits, jnp.int32)
    flags = [jnp.any(over & (numbers == n + 1)) for n in range(len(PAIRS))]
    return sum(flag.astype(jnp.int32) << n for n, flag in enumerate(flags))


def exchange_more(more, wanted, tokens, w_query):
    def branch(bits):
        def run(two, three, tokens, w_query):
            out = []
            for array, at in ((two, 0), (three, 2)):
                pairs = [PAIRS[n] for n in (at, at + 1) if bits >> n & 1]
                moves = [pair for one, other in pairs for pair in ((one, other), (other, one))]
                out.append(lax.ppermute(array, "req", moves) if moves else array)
            return (*out, query_project(tokens, w_query))

        return run

    return lax.switch(wanted, [branch(bits) for bits in range(16)], *more, tokens, w_query)


def query_kernel(tokens_ref, weight_ref, out_ref):
    out_ref[...] = jnp.dot(tokens_ref[...], weight_ref[...], preferred_element_type=jnp.float32)


def query_project(tokens, w_query):
    rows, depth = tokens.shape
    width = w_query.shape[1]
    block = 256
    return pl.pallas_call(
        query_kernel,
        grid=(width // block,),
        in_specs=[
            pl.BlockSpec((rows, depth), lambda i: (0, 0)),
            pl.BlockSpec((depth, block), lambda i: (0, i)),
        ],
        out_specs=pl.BlockSpec((rows, block), lambda i: (0, i)),
        out_shape=jax.ShapeDtypeStruct((rows, width), jnp.float32),
        compiler_params=pltpu.CompilerParams(vmem_limit_bytes=50 * 1024 * 1024),
        cost_estimate=pl.CostEstimate(flops=1024, bytes_accessed=1024, transcendentals=0),
    )(tokens, w_query)


def swap(array, bit):
    return lax.ppermute(array, "cp", [(i, i ^ bit) for i in range(8)])


def add(one, two):
    return one.astype(jnp.float32) + two.astype(jnp.float32)


def halves(send, keep):
    got = swap(send, 1)
    half = keep.shape[2] // 2
    left = [add(keep[n::2, :, :half], got[n::2, :, :half]) for n in (0, 1)]
    right = [
        add(keep[2 * n : 2 * n + 2, :, half:], got[2 * n : 2 * n + 2, :, half:]) for n in (0, 1)
    ]
    return left[0], right[0], left[1].astype(send.dtype), right[1].astype(send.dtype)


def second_level(parts):
    left, right, to_x, to_y = parts
    return add(left, swap(to_x, 2)), add(right, swap(to_y, 4))


def third_level(parts, dtype):
    left, right = parts
    left = add(left[0], swap(left[1].astype(dtype), 4))
    right = add(right[0], swap(right[1].astype(dtype), 2))
    return jnp.concatenate([left, right], axis=1)


def local(
    hidden, residual, w_query, w_keyval, w_out, kv_pool, prefix_len, hit_holder, hit_slot, owner
):
    cp_count = lax.axis_size("cp")
    group_id = lax.axis_index("req")
    cp_rank = lax.axis_index("cp")
    tok_rows = hidden.shape[1]
    stretch_rows = tok_rows * cp_count
    slice_rows = w_keyval.shape[0]
    block_rows = kv_pool.shape[1]
    request_count = hit_holder.shape[0]
    prefix_blocks = hit_holder.shape[1]
    new_blocks = owner.shape[1]
    owner_cap = (new_blocks + 1) // 2
    holder_cap = prefix_blocks // 2
    heads_share = cp_count // KVH
    length = prefix_len[group_id]
    positions = length + jnp.arange(stretch_rows, dtype=jnp.int32)
    cosine, sine = rope_tables(positions)

    group = group_id.reshape(1)
    rank = cp_rank.reshape(1)
    fast = cp_count == 8 and request_count == 4 and block_rows % 16 == 0
    own = hidden[0]
    if fast:
        pool = lax.all_to_all(
            split_heads(kv_pool, own), "cp", split_axis=0, concat_axis=0, tiled=True
        )
        base = holder_cap // 2
        wanted = pairs_wanted(prefix_len, hit_holder, base)
        own, pool, cosine, sine, wanted = lax.optimization_barrier(
            (own, pool, cosine, sine, wanted)
        )
        packed = pack(
            group, rank, hit_holder, hit_slot, pool, w_keyval,
            kv_pool.shape[0], stretch_rows, holder_cap, base,
        )
        main, near, two_more, three_more, *terms = packed
        main = lax.all_to_all(main, "req", split_axis=0, concat_axis=0, tiled=True)
        near = lax.ppermute(near, "req", [(i, i ^ 1) for i in range(4)])
        summed = third_level(second_level(halves(*terms)), terms[0].dtype)
        fresh = finish_fresh(summed, cosine, sine)
        gathered = lax.all_gather(own, "cp", axis=0, tiled=True)
        two, three, raw_queries = exchange_more((two_more, three_more), wanted, gathered, w_query)
        pieces = [pool, main, near, two, three]
    else:
        slot_ids = jnp.arange(holder_cap, dtype=jnp.int32)
        holds_hit = hit_holder == group_id
        hit_order = jnp.cumsum(holds_hit.astype(jnp.int32), axis=1) - 1
        picked = holds_hit[:, None, :] & (hit_order[:, None, :] == slot_ids[None, :, None])
        sources = jnp.sum(jnp.where(picked, hit_slot[:, None, :], 0), axis=2)
        by_head = kv_pool.reshape(-1, block_rows, 2, KVH, HD)[sources]
        by_head = jnp.transpose(by_head, (0, 4, 1, 2, 3, 5))
        sending = jnp.repeat(by_head, heads_share, axis=1).reshape(
            request_count * cp_count, holder_cap * block_rows, 2 * HD
        )
        arrived = lax.all_to_all(sending, ("req", "cp"), split_axis=0, concat_axis=0, tiled=True)
        arrived = arrived.reshape(request_count, cp_count, holder_cap, block_rows, 2 * HD)
        my_holders = hit_holder[group_id]
        hit_index = jnp.arange(prefix_blocks, dtype=jnp.int32)
        earlier = (my_holders[:, None] == my_holders[None, :]) & (
            hit_index[:, None] > hit_index[None, :]
        )
        hit_rank = jnp.sum(earlier.astype(jnp.int32), axis=1)
        pieces = [arrived[my_holders, :, hit_rank].reshape(prefix_blocks * BLK, 2 * HD)]

        gathered = lax.all_gather(own, "cp", axis=0, tiled=True)
        raw_queries = jnp.dot(gathered, w_query, preferred_element_type=jnp.float32)
        columns = lax.dynamic_slice_in_dim(gathered, cp_rank * slice_rows, slice_rows, 1)
        partial_kv = jnp.dot(columns, w_keyval, preferred_element_type=jnp.float32)
        partial_kv = jnp.transpose(
            partial_kv.reshape(stretch_rows, 2, KVH, HD), (2, 0, 1, 3)
        ).reshape(KVH, stretch_rows, 2 * HD)
        partial_kv = jnp.repeat(partial_kv, heads_share, axis=0)
        summed = lax.psum_scatter(partial_kv, "cp", scatter_dimension=0, tiled=True)[0]
        keys = summed[:, :HD]
        keys = keys * cosine + jnp.roll(keys, HD // 2, axis=1) * sine
        fresh = jnp.concatenate([keys, summed[:, HD:]], axis=1).astype(jnp.bfloat16)
    outs = attention(
        prefix_len, group, rank, hit_holder, hit_slot, raw_queries, cosine, sine, fresh, pieces,
        w_out if fast else None,
    )
    my_owners = owner[group_id]
    block_ids = jnp.arange(new_blocks, dtype=jnp.int32)
    before = (my_owners[:, None] == my_owners[None, :]) & (block_ids[:, None] > block_ids[None, :])
    owner_rank = jnp.sum(before.astype(jnp.int32), axis=1)
    targets = jnp.arange(request_count, dtype=jnp.int32)[:, None, None]
    cap_ids = jnp.arange(owner_cap, dtype=jnp.int32)[None, :, None]
    chosen = (my_owners[None, None, :] == targets) & (owner_rank[None, None, :] == cap_ids)
    block_pick = jnp.sum(jnp.where(chosen, block_ids[None, None, :], 0), axis=2)
    present = jnp.any(chosen, axis=2)
    blocks = fresh.reshape(new_blocks, cp_count, block_rows, 2 * HD)[block_pick]
    blocks = jnp.where(present[:, :, None, None, None], blocks, jnp.zeros((), jnp.bfloat16))
    blocks = jnp.transpose(blocks, (0, 2, 1, 3, 4)).reshape(
        request_count * cp_count, owner_cap * block_rows, 2 * HD
    )

    if fast:
        send0, send1, keep0, keep1 = outs
        terms = [halves(send0, keep0), halves(send1, keep1)]
        blocks, terms[1] = lax.optimization_barrier((blocks, terms[1]))
        terms = [second_level(term) for term in terms]
        projected = jnp.concatenate([third_level(term, jnp.bfloat16) for term in terms], axis=1)
    else:
        (attended,) = outs
        projected = lax.psum_scatter(
            jnp.dot(attended, w_out, preferred_element_type=jnp.float32).astype(jnp.bfloat16),
            "cp",
            scatter_dimension=0,
            tiled=True,
        ).astype(jnp.float32)
    layer_out = (residual[0].astype(jnp.float32) + projected).astype(jnp.bfloat16)[None]

    landed = lax.all_to_all(blocks, ("req", "cp"), split_axis=0, concat_axis=0, tiled=True)
    landed = landed.reshape(request_count, cp_count, owner_cap, block_rows, 2, HD)[:, ::heads_share]
    new_cache = jnp.transpose(landed, (0, 2, 3, 4, 1, 5)).reshape(
        1, request_count * owner_cap, block_rows, 2 * KVH * HD
    )
    return (layer_out, new_cache)


def solution(mesh):
    in_specs = (
        P("req", "cp", None),
        P("req", "cp", None),
        P(None, "cp"),
        P("cp", None),
        P("cp", None),
        P("req", "cp", None),
        P(),
        P(),
        P(),
        P(),
    )
    out_specs = (P("req", "cp", None), P("req", None, "cp", None))
    return jax.shard_map(local, mesh=mesh, in_specs=in_specs, out_specs=out_specs, check_vma=False)
```

```python
import functools
import math

import jax
import jax.numpy as jnp
from jax import lax
from jax.experimental import pallas as pl
from jax.experimental.pallas import tpu as pltpu
from jax.sharding import PartitionSpec as P

KVH = 8
HD = 128
BLK = 128
LOG2E = 1.4426950408889634


def frequencies(width):
    half_width = width // 2
    base_freq = jnp.power(
        jnp.float32(500000.0), -jnp.arange(half_width, dtype=jnp.float32) * (2.0 / width)
    )
    wavelength = 2.0 * math.pi / base_freq
    blended = (8192.0 / wavelength - 1.0) / 3.0
    middle = (1.0 - blended) * base_freq / 8.0 + blended * base_freq
    return jnp.where(
        wavelength < 2048.0, base_freq, jnp.where(wavelength > 8192.0, base_freq / 8.0, middle)
    )


def rope_tables(positions):
    angles = positions.astype(jnp.float32)[:, None] * frequencies(HD)[None, :]
    cosine, sine = jnp.cos(angles), jnp.sin(angles)
    return jnp.concatenate([cosine, cosine], axis=1), jnp.concatenate([-sine, sine], axis=1)


def split_kernel(pool_ref, hidden_ref, out_ref):
    key_width = KVH * HD
    slots, block_rows, _ = pool_ref.shape
    width = out_ref.shape[3]

    def one(slot, carry):
        rows = pool_ref[slot]
        for head in range(KVH):
            at = head * HD
            out_ref[head, slot] = jnp.concatenate(
                [rows[:, at : at + HD], rows[:, key_width + at : key_width + at + HD]], axis=1
            )
        return carry

    lax.fori_loop(0, slots, one, 0)
    rows, features = hidden_ref.shape
    share = features // KVH
    for dest in range(KVH):
        for chunk in range(share // width):
            at = dest * share + chunk * width
            for r in range(rows // block_rows):
                out_ref[dest, slots + chunk * (rows // block_rows) + r] = hidden_ref[
                    r * block_rows : (r + 1) * block_rows, at : at + width
                ]


def split_heads(kv_pool, own):
    slots, block_rows, _ = kv_pool.shape
    extra = own.size // (KVH * block_rows * 2 * HD)
    shape = (KVH, slots + extra, block_rows, 2 * HD)
    return pl.pallas_call(
        split_kernel,
        grid=(1,),
        in_specs=[
            pl.BlockSpec(kv_pool.shape, lambda i: (0, 0, 0)),
            pl.BlockSpec(own.shape, lambda i: (0, 0)),
        ],
        out_specs=pl.BlockSpec(shape, lambda i: (0, 0, 0, 0)),
        out_shape=jax.ShapeDtypeStruct(shape, kv_pool.dtype),
        compiler_params=pltpu.CompilerParams(vmem_limit_bytes=52 * 1024 * 1024),
    )(kv_pool, own)


def pack_kernel(
    slots, group_ref, rank_ref, holder_ref, slot_ref, mixed_ref, source_ref,
    main_out, near_out, two_out, three_out, send_ref, keep_ref,
    table_ref, pool_ref, weight_ref, main_ref, near_ref, two_ref, three_ref,
    pool_sems, weight_sems, out_sems,
):
    ranks, groups, block_rows, _ = pool_ref.shape
    pool_copies = [
        pltpu.make_async_copy(mixed_ref.at[r], pool_ref.at[r], pool_sems.at[r])
        for r in range(ranks)
    ]
    share = weight_ref.shape[0] // ranks
    weight_copies = [
        pltpu.make_async_copy(
            source_ref.at[r * share : (r + 1) * share],
            weight_ref.at[r * share : (r + 1) * share],
            weight_sems.at[r],
        )
        for r in range(ranks)
    ]
    for copy in pool_copies + weight_copies:
        copy.start()
    group = group_ref[0]
    base = main_ref.shape[1]
    cap = base + near_ref.shape[0]
    for n in range(3 * cap):
        table_ref[n] = 0
    for n in range(3):
        request = group ^ (n + 1)

        def one(index, count, n=n, request=request):
            mine = holder_ref[request, index] == group
            at = jnp.where(mine, n * cap + count, 3 * cap)
            table_ref[at] = slot_ref[request, index]
            return count + mine.astype(jnp.int32)

        lax.fori_loop(0, holder_ref.shape[1], one, jnp.int32(0), unroll=True)
    for copy in pool_copies:
        copy.wait()
    for n, more_ref in enumerate((near_ref, two_ref, three_ref)):
        for at in range(cap):
            slot = table_ref[n * cap + at]
            for r in range(ranks):
                rows = slice(r * block_rows, (r + 1) * block_rows)
                if at < base:
                    main_ref[group ^ (n + 1), at, rows, :] = pool_ref[r, slot]
                else:
                    more_ref[at - base, rows, :] = pool_ref[r, slot]
    out_copies = [
        pltpu.make_async_copy(main_ref.at[r], main_out.at[r], out_sems.at[3 + r])
        for r in range(main_ref.shape[0])
    ] + [
        pltpu.make_async_copy(one, out, out_sems.at[n])
        for n, (one, out) in enumerate(
            ((near_ref, near_out), (two_ref, two_out), (three_ref, three_out))
        )
    ]
    for copy in out_copies:
        copy.start()

    tall = send_ref.shape[1] // ranks // block_rows
    tokens = jnp.concatenate(
        [
            jnp.concatenate([pool_ref[r, at + i] for at in range(slots, groups, tall)], axis=1)
            for r in range(ranks)
            for i in range(tall)
        ],
        axis=0,
    )
    for copy in weight_copies:
        copy.wait()
    key_width = KVH * HD
    whole = jnp.dot(tokens, weight_ref[...], preferred_element_type=jnp.float32)
    whole = whole.astype(send_ref.dtype)
    for head in range(KVH):
        at = head * HD
        product = jnp.concatenate(
            [whole[:, at : at + HD], whole[:, key_width + at : key_width + at + HD]], axis=1
        )
        distance = head ^ rank_ref[0]

        @pl.when(distance % 2 == 1)
        def _(product=product, distance=distance):
            send_ref[distance // 2] = product

        @pl.when(distance % 2 == 0)
        def _(product=product, distance=distance):
            keep_ref[distance // 2] = product

    for copy in out_copies:
        copy.wait()


def pack(group, rank, hit_holder, hit_slot, mixed, w_keyval, slots, tokens, cap, base):
    ranks, _, block_rows, width = mixed.shape
    requests = hit_holder.shape[0]
    block = (ranks * block_rows, width)
    shapes = [(requests, base, *block)] + [(cap - base, *block)] * 3
    terms = [(KVH // 2, tokens, width)] * 2
    anywhere = pl.BlockSpec(memory_space=pl.ANY)
    return pl.pallas_call(
        functools.partial(pack_kernel, slots),
        grid_spec=pltpu.PrefetchScalarGridSpec(
            num_scalar_prefetch=4,
            grid=(1,),
            in_specs=[anywhere] * 2,
            out_specs=[anywhere] * 4 + [pl.BlockSpec(shape, lambda i, *_: (0, 0, 0)) for shape in terms],
            scratch_shapes=[pltpu.SMEM((3 * cap + 1,), jnp.int32)]
            + [pltpu.VMEM(array.shape, mixed.dtype) for array in (mixed, w_keyval)]
            + [pltpu.VMEM(shape, mixed.dtype) for shape in shapes]
            + [pltpu.SemaphoreType.DMA((n,)) for n in (ranks, ranks, 3 + requests)],
        ),
        out_shape=[jax.ShapeDtypeStruct(shape, mixed.dtype) for shape in shapes + terms],
        compiler_params=pltpu.CompilerParams(vmem_limit_bytes=24 * 1024 * 1024),
    )(group, rank, hit_holder, hit_slot, mixed, w_keyval)


def fresh_kernel(group_ref, owner_ref, summed_ref, cos_ref, sin_ref, fresh_ref, sends_ref):
    keys = summed_ref[:, :HD]
    keys = keys * cos_ref[...] + pltpu.roll(keys, HD // 2, 1) * sin_ref[...]
    fresh_ref[:, :HD] = keys.astype(jnp.bfloat16)
    fresh_ref[:, HD:] = summed_ref[:, HD:].astype(jnp.bfloat16)
    sends_ref[...] = jnp.zeros_like(sends_ref)
    _, ranks, rows, _ = sends_ref.shape
    for block in range(owner_ref.shape[1]):
        for r in range(ranks):
            at = block * BLK + r * rows
            sends_ref[owner_ref[group_ref[0], block], r] = fresh_ref[at : at + rows, :]


def finish_fresh(group, owner, summed, cosine, sine, ranks):
    shapes = [summed.shape, (owner.shape[0], ranks, BLK // ranks, summed.shape[1])]
    return pl.pallas_call(
        fresh_kernel,
        grid_spec=pltpu.PrefetchScalarGridSpec(
            num_scalar_prefetch=2,
            grid=(1,),
            in_specs=[
                pl.BlockSpec(array.shape, lambda i, *_: (0, 0)) for array in (summed, cosine, sine)
            ],
            out_specs=[
                pl.BlockSpec(shape, lambda i, *_, n=len(shape): (0,) * n) for shape in shapes
            ],
        ),
        out_shape=[jax.ShapeDtypeStruct(shape, jnp.bfloat16) for shape in shapes],
    )(group, owner, summed, cosine, sine)


def place_pieces(group, length, holder_ref, slot_ref, refs, prefix_ref):
    pool_ref, main_ref, near_ref, two_ref, three_ref = refs
    ranks, _, block_rows, _ = pool_ref.shape
    rows = ranks * block_rows
    base = main_ref.shape[1]

    def one(index, counts):
        holder = holder_ref[group, index]
        distance = holder ^ group
        count = sum(jnp.where(distance == d, counts[d], 0) for d in range(4))
        at = pl.multiple_of(index * rows, rows)
        seen = index * rows < length

        @pl.when(jnp.logical_not(seen))
        def _():
            prefix_ref[pl.ds(at, rows), :] = jnp.zeros((rows, 2 * HD), jnp.bfloat16)

        @pl.when(seen & (distance == 0))
        def _():
            slot = slot_ref[group, index]
            for r in range(ranks):
                prefix_ref[pl.ds(at + r * block_rows, block_rows), :] = pool_ref[r, slot]

        low = count < base
        rest = count - base

        @pl.when(seen & (distance != 0) & low)
        def _():
            prefix_ref[pl.ds(at, rows), :] = main_ref[holder, count]

        def take(when, ref, n):
            @pl.when(seen & when)
            def _():
                prefix_ref[pl.ds(at, rows), :] = ref[n]

        take((distance == 1) & ~low, near_ref, rest)
        take((distance == 2) & ~low, two_ref, rest)
        take((distance == 3) & ~low, three_ref, rest)
        return tuple(n + (distance == d).astype(jnp.int32) for d, n in enumerate(counts))

    lax.fori_loop(0, holder_ref.shape[1], one, (jnp.int32(0),) * 4)


def attention_kernel(
    tile, ordered, length_ref, group_ref, rank_ref, holder_ref, slot_ref, q_ref, cos_ref, sin_ref, fresh_ref, *refs
):
    if ordered:
        *piece_refs, out_ref, prefix_ref = refs
    else:
        *piece_refs, weight_ref, send0, send1, keep0, keep1 = refs[:-5]
        prefix_ref, out_ref, rows_ref, held_ref, arrived = refs[-5:]
        fetch = pltpu.make_async_copy(weight_ref, held_ref, arrived)

        @pl.when(pl.program_id(0) == 0)
        def _():
            fetch.start()

    group = group_ref[0]
    span = prefix_ref.shape[0]
    row0 = pl.program_id(1) * tile

    @pl.when((pl.program_id(0) == 0) & (pl.program_id(1) == 0))
    def _():
        if ordered:
            prefix_ref[...] = piece_refs[0][...]
        else:
            place_pieces(group, length_ref[group], holder_ref, slot_ref, piece_refs, prefix_ref)

    seen = lax.broadcasted_iota(jnp.int32, (1, span), 1) < length_ref[group]
    bias = jnp.where(seen, 0.0, -1e30)
    columns = lax.broadcasted_iota(jnp.int32, (tile, fresh_ref.shape[0]), 1)
    rows = lax.broadcasted_iota(jnp.int32, (tile, fresh_ref.shape[0]), 0) + row0
    causal = columns <= rows
    cosine = cos_ref[pl.ds(pl.multiple_of(row0, tile), tile), :]
    sine = sin_ref[pl.ds(pl.multiple_of(row0, tile), tile), :]
    factor = HD ** (-0.5) * LOG2E

    def scores(query, keys):
        return lax.dot_general(
            query, keys, (((1,), (1,)), ((), ())), preferred_element_type=jnp.float32
        )

    for head in range(q_ref.shape[1] // HD):
        lanes = slice(head * HD, (head + 1) * HD)
        raw = q_ref[:, lanes]
        query = raw * cosine + pltpu.roll(raw, HD // 2, 1) * sine
        query = (query * factor).astype(jnp.bfloat16)
        old = scores(query, prefix_ref[:, :HD]) + bias
        new = jnp.where(causal, scores(query, fresh_ref[:, :HD]), -1e30)
        peak = jnp.maximum(
            jnp.max(old, axis=1, keepdims=True), jnp.max(new, axis=1, keepdims=True)
        )
        old, new = jnp.exp2(old - peak), jnp.exp2(new - peak)
        total = jnp.sum(old, axis=1, keepdims=True) + jnp.sum(new, axis=1, keepdims=True)
        mixed = jnp.dot(
            old.astype(jnp.bfloat16), prefix_ref[:, HD:], preferred_element_type=jnp.float32
        ) + jnp.dot(
            new.astype(jnp.bfloat16), fresh_ref[:, HD:], preferred_element_type=jnp.float32
        )
        mixed = (mixed / total).astype(jnp.bfloat16)
        if ordered:
            out_ref[:, lanes] = mixed
        else:
            out_ref[pl.program_id(0) * (q_ref.shape[1] // HD) + head] = mixed

    if not ordered:

        @pl.when(pl.program_id(0) == pl.num_programs(0) - 1)
        def _():
            fetch.wait()
            project_kernel(rank_ref[0], out_ref, rows_ref, held_ref, (send0, send1, keep0, keep1))


def project_kernel(rank, heads_ref, rows_ref, weight_ref, out_refs):
    quads, rows, width = out_refs[0].shape
    for head in range(heads_ref.shape[0]):
        for n in range(2 * quads):
            source = rank ^ (n % quads * 2) ^ (1 - n // quads)
            at = pl.multiple_of(source * rows, rows)
            rows_ref[n * rows : (n + 1) * rows, head * HD : (head + 1) * HD] = heads_ref[
                head, pl.ds(at, rows), :
            ]
    block = 1024
    for half in range(2):

        def one(step, carry, half=half):
            at = pl.multiple_of(step * block, block)
            source = pl.multiple_of(half * width + at, block)
            product = jnp.dot(
                rows_ref[...],
                weight_ref[:, pl.ds(source, block)],
                preferred_element_type=jnp.float32,
            ).astype(jnp.bfloat16)
            for n in range(quads):
                out_refs[half][n, :, pl.ds(at, block)] = product[n * rows : (n + 1) * rows]
                out_refs[2 + half][n, :, pl.ds(at, block)] = product[
                    (quads + n) * rows : (quads + n + 1) * rows
                ]
            return carry

        lax.fori_loop(0, width // block, one, 0)


def attention(
    prefix_len, group, rank, hit_holder, hit_slot, raw_queries, cosine, sine, fresh, pieces, w_out
):
    rows, width = raw_queries.shape
    tile = min(256, rows)
    span = hit_holder.shape[1] * BLK
    keys = span + rows
    ordered = w_out is None
    fixed = [cosine, sine, fresh, *pieces]

    def whole(array):
        return pl.BlockSpec(
            array.shape, lambda h, t, *_: (0,) * len(array.shape), pipeline_mode=pl.Buffered(1)
        )

    scratch = [pltpu.VMEM((span, 2 * HD), jnp.bfloat16)]
    in_specs = [pl.BlockSpec((tile, 2 * HD), lambda h, t, *_: (t, h))]
    in_specs += [whole(array) for array in fixed]
    if ordered:
        outs = [jax.ShapeDtypeStruct((rows, width), jnp.bfloat16)]
        out_specs = [pl.BlockSpec((tile, 2 * HD), lambda h, t, *_: (t, h))]
    else:
        fixed.append(w_out)
        in_specs.append(pl.BlockSpec(memory_space=pl.ANY))
        part = (4, rows // 8, w_out.shape[1] // 2)
        outs = [jax.ShapeDtypeStruct(part, jnp.bfloat16)] * 4
        out_specs = [pl.BlockSpec(part, lambda h, t, *_: (0, 0, 0))] * 4
        scratch += [
            pltpu.VMEM((width // HD, rows, HD), jnp.bfloat16),
            pltpu.VMEM((rows, width), jnp.bfloat16),
            pltpu.VMEM(w_out.shape, jnp.bfloat16),
            pltpu.SemaphoreType.DMA,
        ]
    return pl.pallas_call(
        functools.partial(attention_kernel, tile, ordered),
        grid_spec=pltpu.PrefetchScalarGridSpec(
            num_scalar_prefetch=5,
            grid=(width // (2 * HD), rows // tile),
            in_specs=in_specs,
            out_specs=out_specs,
            scratch_shapes=scratch,
        ),
        out_shape=outs,
        compiler_params=pltpu.CompilerParams(vmem_limit_bytes=60 * 1024 * 1024),
        cost_estimate=pl.CostEstimate(
            flops=4 * rows * width * keys,
            bytes_accessed=rows * width * 6,
            transcendentals=rows * width // HD * keys,
        ),
    )(prefix_len, group, rank, hit_holder, hit_slot, raw_queries, *fixed)


PAIRS = ((0, 2), (1, 3), (0, 3), (1, 2))


def pairs_wanted(prefix_len, hit_holder, base):
    requests, blocks = hit_holder.shape
    starts = jnp.arange(blocks, dtype=jnp.int32) * BLK
    seen = starts[None, :] < prefix_len[:, None]
    holders = jnp.arange(requests, dtype=jnp.int32)
    held = (hit_holder[:, None, :] == holders[None, :, None]) & seen[:, None, :]
    over = jnp.sum(held.astype(jnp.int32), axis=2) > base
    bits = [[0] * requests for _ in range(requests)]
    for n, (one, other) in enumerate(PAIRS):
        bits[one][other] = bits[other][one] = n + 1
    numbers = jnp.asarray(bits, jnp.int32)
    flags = [jnp.any(over & (numbers == n + 1)) for n in range(len(PAIRS))]
    return sum(flag.astype(jnp.int32) << n for n, flag in enumerate(flags))


def exchange_more(more, wanted, tokens, w_query):
    def branch(bits):
        def run(two, three, tokens, w_query):
            out = []
            for array, at in ((two, 0), (three, 2)):
                pairs = [PAIRS[n] for n in (at, at + 1) if bits >> n & 1]
                moves = [pair for one, other in pairs for pair in ((one, other), (other, one))]
                out.append(lax.ppermute(array, "req", moves) if moves else array)
            return (*out, query_project(tokens, w_query))

        return run

    return lax.switch(wanted, [branch(bits) for bits in range(16)], *more, tokens, w_query)


def query_kernel(tokens_ref, weight_ref, out_ref):
    out_ref[...] = jnp.dot(tokens_ref[...], weight_ref[...], preferred_element_type=jnp.float32)


def query_project(tokens, w_query):
    rows, depth = tokens.shape
    width = w_query.shape[1]
    block = 256
    return pl.pallas_call(
        query_kernel,
        grid=(width // block,),
        in_specs=[
            pl.BlockSpec((rows, depth), lambda i: (0, 0)),
            pl.BlockSpec((depth, block), lambda i: (0, i)),
        ],
        out_specs=pl.BlockSpec((rows, block), lambda i: (0, i)),
        out_shape=jax.ShapeDtypeStruct((rows, width), jnp.float32),
        compiler_params=pltpu.CompilerParams(vmem_limit_bytes=50 * 1024 * 1024),
        cost_estimate=pl.CostEstimate(flops=1024, bytes_accessed=1024, transcendentals=0),
    )(tokens, w_query)


def swap(array, bit):
    return lax.ppermute(array, "cp", [(i, i ^ bit) for i in range(8)])


def add(one, two):
    return one.astype(jnp.float32) + two.astype(jnp.float32)


VMEM_REF = pl.BlockSpec(memory_space=pltpu.VMEM)


def pair_kernel(near, keep_ref, got_ref, kept_ref, sent_ref):
    for n in range(2):
        stays, goes = (2 * n, 2 * n + 1) if near else (n, n + 2)
        kept_ref[n] = add(keep_ref[stays], got_ref[stays])
        sent_ref[n] = add(keep_ref[goes], got_ref[goes]).astype(sent_ref.dtype)


def pair_sum(keep, got, near):
    half = (2, *keep.shape[1:])
    outs = [jax.ShapeDtypeStruct(half, jnp.float32), jax.ShapeDtypeStruct(half, keep.dtype)]
    return pl.pallas_call(
        functools.partial(pair_kernel, near),
        in_specs=[VMEM_REF] * 2,
        out_specs=[VMEM_REF] * len(outs),
        out_shape=outs,
        compiler_params=pltpu.CompilerParams(vmem_limit_bytes=8 * 1024 * 1024),
    )(keep, got)


def level_kernel(kept_ref, got_ref, *refs):
    refs[-2][...] = add(kept_ref[0], got_ref[0])
    refs[-1][...] = add(kept_ref[1], got_ref[1]).astype(got_ref.dtype)
    if len(refs) > 2:
        refs[1][...] = refs[0][...]


def second_level(kept, sent, bit, *blocks):
    shape = kept.shape[1:]
    outs = [jax.ShapeDtypeStruct(array.shape, array.dtype) for array in blocks]
    outs += [jax.ShapeDtypeStruct(shape, jnp.float32), jax.ShapeDtypeStruct(shape, sent.dtype)]
    *blocks, kept, sent = pl.pallas_call(
        level_kernel,
        in_specs=[VMEM_REF] * (2 + len(blocks)),
        out_specs=[VMEM_REF] * len(outs),
        out_shape=outs,
        compiler_params=pltpu.CompilerParams(vmem_limit_bytes=8 * 1024 * 1024),
    )(kept, swap(sent, bit), *blocks)
    return *blocks, kept, swap(sent, 6 - bit)


def last_kernel(residual_ref, *refs):
    left, got_left, right, got_right, landed_ref, out_ref, cache_ref = refs
    half = left.shape[1]
    out_ref[0, :, :half] = (add(left[...], got_left[...]) + residual_ref[:, :half]).astype(
        jnp.bfloat16
    )
    out_ref[0, :, half:] = (add(right[...], got_right[...]) + residual_ref[:, half:]).astype(
        jnp.bfloat16
    )
    key_width = KVH * HD
    for source in range(cache_ref.shape[1]):
        for head in range(KVH):
            rows = landed_ref[source, head]
            at = head * HD
            cache_ref[0, source, :, at : at + HD] = rows[:, :HD]
            cache_ref[0, source, :, key_width + at : key_width + at + HD] = rows[:, HD:]


def last_sums(residual, left, right, landed, cache_shape):
    shapes = [(1, *residual.shape), cache_shape]
    return pl.pallas_call(
        last_kernel,
        grid=(1,),
        in_specs=[VMEM_REF] * 6,
        out_specs=[pl.BlockSpec(shape, lambda i, n=len(shape): (0,) * n) for shape in shapes],
        out_shape=[jax.ShapeDtypeStruct(shape, jnp.bfloat16) for shape in shapes],
        compiler_params=pltpu.CompilerParams(vmem_limit_bytes=12 * 1024 * 1024),
    )(residual, *left, *right, landed)


def local(
    hidden, residual, w_query, w_keyval, w_out, kv_pool, prefix_len, hit_holder, hit_slot, owner
):
    cp_count = lax.axis_size("cp")
    group_id = lax.axis_index("req")
    cp_rank = lax.axis_index("cp")
    tok_rows = hidden.shape[1]
    stretch_rows = tok_rows * cp_count
    slice_rows = w_keyval.shape[0]
    block_rows = kv_pool.shape[1]
    request_count = hit_holder.shape[0]
    prefix_blocks = hit_holder.shape[1]
    new_blocks = owner.shape[1]
    owner_cap = (new_blocks + 1) // 2
    holder_cap = prefix_blocks // 2
    heads_share = cp_count // KVH
    length = prefix_len[group_id]
    positions = length + jnp.arange(stretch_rows, dtype=jnp.int32)
    cosine, sine = rope_tables(positions)

    group = group_id.reshape(1)
    rank = cp_rank.reshape(1)
    fast = cp_count == 8 and request_count == 4 and owner_cap == 1 and block_rows % 16 == 0
    own = hidden[0]
    if fast:
        pool = lax.all_to_all(
            split_heads(kv_pool, own), "cp", split_axis=0, concat_axis=0, tiled=True
        )
        base = holder_cap // 2
        wanted = pairs_wanted(prefix_len, hit_holder, base)
        own, pool, cosine, sine, wanted = lax.optimization_barrier(
            (own, pool, cosine, sine, wanted)
        )
        packed = pack(
            group, rank, hit_holder, hit_slot, pool, w_keyval,
            kv_pool.shape[0], stretch_rows, holder_cap, base,
        )
        main, near, two_more, three_more, *terms = packed
        main = lax.all_to_all(main, "req", split_axis=0, concat_axis=0, tiled=True)
        near = lax.ppermute(near, "req", [(i, i ^ 1) for i in range(4)])
        send, keep = terms
        got = swap(send, 1)
        key_terms = second_level(*pair_sum(keep[..., :HD], got[..., :HD], True), 2)
        value_terms = second_level(*pair_sum(keep[..., HD:], got[..., HD:], False), 4)
        summed = jnp.concatenate([add(*key_terms), add(*value_terms)], axis=1)
        fresh, blocks = finish_fresh(group, owner, summed, cosine, sine, cp_count)
        gathered = lax.all_gather(own, "cp", axis=0, tiled=True)
        two, three, raw_queries = exchange_more((two_more, three_more), wanted, gathered, w_query)
        pieces = [pool, main, near, two, three]
    else:
        slot_ids = jnp.arange(holder_cap, dtype=jnp.int32)
        holds_hit = hit_holder == group_id
        hit_order = jnp.cumsum(holds_hit.astype(jnp.int32), axis=1) - 1
        picked = holds_hit[:, None, :] & (hit_order[:, None, :] == slot_ids[None, :, None])
        sources = jnp.sum(jnp.where(picked, hit_slot[:, None, :], 0), axis=2)
        by_head = kv_pool.reshape(-1, block_rows, 2, KVH, HD)[sources]
        by_head = jnp.transpose(by_head, (0, 4, 1, 2, 3, 5))
        sending = jnp.repeat(by_head, heads_share, axis=1).reshape(
            request_count * cp_count, holder_cap * block_rows, 2 * HD
        )
        arrived = lax.all_to_all(sending, ("req", "cp"), split_axis=0, concat_axis=0, tiled=True)
        arrived = arrived.reshape(request_count, cp_count, holder_cap, block_rows, 2 * HD)
        my_holders = hit_holder[group_id]
        hit_index = jnp.arange(prefix_blocks, dtype=jnp.int32)
        earlier = (my_holders[:, None] == my_holders[None, :]) & (
            hit_index[:, None] > hit_index[None, :]
        )
        hit_rank = jnp.sum(earlier.astype(jnp.int32), axis=1)
        pieces = [arrived[my_holders, :, hit_rank].reshape(prefix_blocks * BLK, 2 * HD)]

        gathered = lax.all_gather(own, "cp", axis=0, tiled=True)
        raw_queries = jnp.dot(gathered, w_query, preferred_element_type=jnp.float32)
        columns = lax.dynamic_slice_in_dim(gathered, cp_rank * slice_rows, slice_rows, 1)
        partial_kv = jnp.dot(columns, w_keyval, preferred_element_type=jnp.float32)
        partial_kv = jnp.transpose(
            partial_kv.reshape(stretch_rows, 2, KVH, HD), (2, 0, 1, 3)
        ).reshape(KVH, stretch_rows, 2 * HD)
        partial_kv = jnp.repeat(partial_kv, heads_share, axis=0)
        summed = lax.psum_scatter(partial_kv, "cp", scatter_dimension=0, tiled=True)[0]
        keys = summed[:, :HD]
        keys = keys * cosine + jnp.roll(keys, HD // 2, axis=1) * sine
        fresh = jnp.concatenate([keys, summed[:, HD:]], axis=1).astype(jnp.bfloat16)
    outs = attention(
        prefix_len, group, rank, hit_holder, hit_slot, raw_queries, cosine, sine, fresh, pieces,
        w_out if fast else None,
    )
    if fast:
        send0, send1, keep0, keep1 = outs
        blocks, *left = second_level(*pair_sum(keep0, swap(send0, 1), True), 2, blocks)
        right = second_level(*pair_sum(keep1, swap(send1, 1), False), 4)
        blocks = blocks.reshape(-1, *blocks.shape[2:])
        landed = lax.all_to_all(blocks, ("req", "cp"), split_axis=0, concat_axis=0, tiled=True)
        landed = landed.reshape(request_count, cp_count, block_rows, 2 * HD)
        cache_shape = (1, request_count, block_rows, 2 * KVH * HD)
        return tuple(last_sums(residual[0], left, right, landed, cache_shape))
    (attended,) = outs
    projected = lax.psum_scatter(
        jnp.dot(attended, w_out, preferred_element_type=jnp.float32).astype(jnp.bfloat16),
        "cp",
        scatter_dimension=0,
        tiled=True,
    ).astype(jnp.float32)
    layer_out = (residual[0].astype(jnp.float32) + projected).astype(jnp.bfloat16)[None]

    my_owners = owner[group_id]
    block_ids = jnp.arange(new_blocks, dtype=jnp.int32)
    before = (my_owners[:, None] == my_owners[None, :]) & (block_ids[:, None] > block_ids[None, :])
    owner_rank = jnp.sum(before.astype(jnp.int32), axis=1)
    targets = jnp.arange(request_count, dtype=jnp.int32)[:, None, None]
    cap_ids = jnp.arange(owner_cap, dtype=jnp.int32)[None, :, None]
    chosen = (my_owners[None, None, :] == targets) & (owner_rank[None, None, :] == cap_ids)
    block_pick = jnp.sum(jnp.where(chosen, block_ids[None, None, :], 0), axis=2)
    present = jnp.any(chosen, axis=2)
    blocks = fresh.reshape(new_blocks, cp_count, block_rows, 2 * HD)[block_pick]
    blocks = jnp.where(present[:, :, None, None, None], blocks, jnp.zeros((), jnp.bfloat16))
    blocks = jnp.transpose(blocks, (0, 2, 1, 3, 4)).reshape(
        request_count * cp_count, owner_cap * block_rows, 2 * HD
    )
    landed = lax.all_to_all(blocks, ("req", "cp"), split_axis=0, concat_axis=0, tiled=True)
    landed = landed.reshape(request_count, cp_count, owner_cap, block_rows, 2, HD)[:, ::heads_share]
    new_cache = jnp.transpose(landed, (0, 2, 3, 4, 1, 5)).reshape(
        1, request_count * owner_cap, block_rows, 2 * KVH * HD
    )
    return (layer_out, new_cache)


def solution(mesh):
    in_specs = (
        P("req", "cp", None),
        P("req", "cp", None),
        P(None, "cp"),
        P("cp", None),
        P("cp", None),
        P("req", "cp", None),
        P(),
        P(),
        P(),
        P(),
    )
    out_specs = (P("req", "cp", None), P("req", None, "cp", None))
    return jax.shard_map(local, mesh=mesh, in_specs=in_specs, out_specs=out_specs, check_vma=False)
```

```python
import functools
import math

import jax
import jax.numpy as jnp
from jax import lax
from jax.experimental import pallas as pl
from jax.experimental.pallas import tpu as pltpu
from jax.sharding import PartitionSpec as P

KVH = 8
HD = 128
BLK = 128
LOG2E = 1.4426950408889634


def frequencies(width):
    half_width = width // 2
    base_freq = jnp.power(
        jnp.float32(500000.0), -jnp.arange(half_width, dtype=jnp.float32) * (2.0 / width)
    )
    wavelength = 2.0 * math.pi / base_freq
    blended = (8192.0 / wavelength - 1.0) / 3.0
    middle = (1.0 - blended) * base_freq / 8.0 + blended * base_freq
    return jnp.where(
        wavelength < 2048.0, base_freq, jnp.where(wavelength > 8192.0, base_freq / 8.0, middle)
    )


def rope_tables(positions):
    angles = positions.astype(jnp.float32)[:, None] * frequencies(HD)[None, :]
    cosine, sine = jnp.cos(angles), jnp.sin(angles)
    return jnp.concatenate([cosine, cosine], axis=1), jnp.concatenate([-sine, sine], axis=1)


def split_kernel(pool_in, hidden_in, out, pool_ref, hidden_ref, out_ref, in_sems, out_sems):
    heads, groups, block_rows, width = out_ref.shape
    slots = pool_ref.shape[0]
    rows, features = hidden_ref.shape
    few, tall = slots // 4, rows // block_rows
    copies = [
        pltpu.make_async_copy(
            pool_in.at[n * few : (n + 1) * few], pool_ref.at[n * few : (n + 1) * few], in_sems.at[n]
        )
        for n in range(4)
    ]
    copies.append(pltpu.make_async_copy(hidden_in, hidden_ref, in_sems.at[4]))
    for copy in copies:
        copy.start()
    for copy in copies:
        copy.wait()
    key_width = KVH * HD
    share = features // heads
    copies = [
        pltpu.make_async_copy(out_ref.at[head], out.at[head], out_sems.at[head])
        for head in range(heads)
    ]
    for head in range(heads):
        at = head * HD
        for slot in range(slots):
            out_ref[head, slot, :, :HD] = pool_ref[slot, :, at : at + HD]
            out_ref[head, slot, :, HD:] = pool_ref[slot, :, key_width + at : key_width + at + HD]
        for chunk in range(share // width):
            source = head * share + chunk * width
            for r in range(tall):
                out_ref[head, slots + chunk * tall + r] = hidden_ref[
                    r * block_rows : (r + 1) * block_rows, source : source + width
                ]
        copies[head].start()
    for copy in copies:
        copy.wait()


def split_heads(kv_pool, own):
    slots, block_rows, _ = kv_pool.shape
    extra = own.size // (KVH * block_rows * 2 * HD)
    shape = (KVH, slots + extra, block_rows, 2 * HD)
    anywhere = pl.BlockSpec(memory_space=pl.ANY)
    return pl.pallas_call(
        split_kernel,
        in_specs=[anywhere] * 2,
        out_specs=anywhere,
        out_shape=jax.ShapeDtypeStruct(shape, kv_pool.dtype),
        scratch_shapes=[
            pltpu.VMEM(array, kv_pool.dtype) for array in (kv_pool.shape, own.shape, shape)
        ]
        + [pltpu.SemaphoreType.DMA((n,)) for n in (5, KVH)],
        compiler_params=pltpu.CompilerParams(vmem_limit_bytes=62 * 1024 * 1024),
    )(kv_pool, own)


def pack_kernel(
    slots, group_ref, rank_ref, holder_ref, slot_ref, mixed_ref, source_ref,
    main_out, near_out, two_out, three_out, send_ref, keep_ref,
    table_ref, pool_ref, weight_ref, main_ref, near_ref, two_ref, three_ref,
    pool_sems, weight_sems, out_sems,
):
    ranks, groups, block_rows, _ = pool_ref.shape
    pool_copies = [
        pltpu.make_async_copy(mixed_ref.at[r], pool_ref.at[r], pool_sems.at[r])
        for r in range(ranks)
    ]
    share = weight_ref.shape[0] // ranks
    weight_copies = [
        pltpu.make_async_copy(
            source_ref.at[r * share : (r + 1) * share],
            weight_ref.at[r * share : (r + 1) * share],
            weight_sems.at[r],
        )
        for r in range(ranks)
    ]
    for copy in pool_copies + weight_copies:
        copy.start()
    group = group_ref[0]
    base = main_ref.shape[1]
    cap = base + near_ref.shape[0]
    for n in range(3 * cap):
        table_ref[n] = 0
    for n in range(3):
        request = group ^ (n + 1)

        def one(index, count, n=n, request=request):
            mine = holder_ref[request, index] == group
            at = jnp.where(mine, n * cap + count, 3 * cap)
            table_ref[at] = slot_ref[request, index]
            return count + mine.astype(jnp.int32)

        lax.fori_loop(0, holder_ref.shape[1], one, jnp.int32(0), unroll=True)
    for copy in pool_copies:
        copy.wait()
    for n, more_ref in enumerate((near_ref, two_ref, three_ref)):
        for at in range(cap):
            slot = table_ref[n * cap + at]
            for r in range(ranks):
                rows = slice(r * block_rows, (r + 1) * block_rows)
                if at < base:
                    main_ref[group ^ (n + 1), at, rows, :] = pool_ref[r, slot]
                else:
                    more_ref[at - base, rows, :] = pool_ref[r, slot]
    out_copies = [
        pltpu.make_async_copy(main_ref.at[r], main_out.at[r], out_sems.at[3 + r])
        for r in range(main_ref.shape[0])
    ] + [
        pltpu.make_async_copy(one, out, out_sems.at[n])
        for n, (one, out) in enumerate(
            ((near_ref, near_out), (two_ref, two_out), (three_ref, three_out))
        )
    ]
    for copy in out_copies:
        copy.start()

    tall = send_ref.shape[1] // ranks // block_rows
    tokens = jnp.concatenate(
        [
            jnp.concatenate([pool_ref[r, at + i] for at in range(slots, groups, tall)], axis=1)
            for r in range(ranks)
            for i in range(tall)
        ],
        axis=0,
    )
    for copy in weight_copies:
        copy.wait()
    key_width = KVH * HD
    whole = jnp.dot(tokens, weight_ref[...], preferred_element_type=jnp.float32)
    whole = whole.astype(send_ref.dtype)
    for head in range(KVH):
        at = head * HD
        product = jnp.concatenate(
            [whole[:, at : at + HD], whole[:, key_width + at : key_width + at + HD]], axis=1
        )
        distance = head ^ rank_ref[0]

        @pl.when(distance % 2 == 1)
        def _(product=product, distance=distance):
            send_ref[distance // 2] = product

        @pl.when(distance % 2 == 0)
        def _(product=product, distance=distance):
            keep_ref[distance // 2] = product

    for copy in out_copies:
        copy.wait()


def pack(group, rank, hit_holder, hit_slot, mixed, w_keyval, slots, tokens, cap, base):
    ranks, _, block_rows, width = mixed.shape
    requests = hit_holder.shape[0]
    block = (ranks * block_rows, width)
    shapes = [(requests, base, *block)] + [(cap - base, *block)] * 3
    terms = [(KVH // 2, tokens, width)] * 2
    anywhere = pl.BlockSpec(memory_space=pl.ANY)
    return pl.pallas_call(
        functools.partial(pack_kernel, slots),
        grid_spec=pltpu.PrefetchScalarGridSpec(
            num_scalar_prefetch=4,
            grid=(1,),
            in_specs=[anywhere] * 2,
            out_specs=[anywhere] * 4 + [pl.BlockSpec(shape, lambda i, *_: (0, 0, 0)) for shape in terms],
            scratch_shapes=[pltpu.SMEM((3 * cap + 1,), jnp.int32)]
            + [pltpu.VMEM(array.shape, mixed.dtype) for array in (mixed, w_keyval)]
            + [pltpu.VMEM(shape, mixed.dtype) for shape in shapes]
            + [pltpu.SemaphoreType.DMA((n,)) for n in (ranks, ranks, 3 + requests)],
        ),
        out_shape=[jax.ShapeDtypeStruct(shape, mixed.dtype) for shape in shapes + terms],
        compiler_params=pltpu.CompilerParams(vmem_limit_bytes=59 * 1024 * 1024),
    )(group, rank, hit_holder, hit_slot, mixed, w_keyval)


def fresh_kernel(group_ref, owner_ref, summed_ref, cos_ref, sin_ref, fresh_ref, sends_ref):
    keys = summed_ref[:, :HD]
    keys = keys * cos_ref[...] + pltpu.roll(keys, HD // 2, 1) * sin_ref[...]
    fresh_ref[:, :HD] = keys.astype(jnp.bfloat16)
    fresh_ref[:, HD:] = summed_ref[:, HD:].astype(jnp.bfloat16)
    sends_ref[...] = jnp.zeros_like(sends_ref)
    _, ranks, rows, _ = sends_ref.shape
    for block in range(owner_ref.shape[1]):
        for r in range(ranks):
            at = block * BLK + r * rows
            sends_ref[owner_ref[group_ref[0], block], r] = fresh_ref[at : at + rows, :]


def finish_fresh(group, owner, summed, cosine, sine, ranks):
    shapes = [summed.shape, (owner.shape[0], ranks, BLK // ranks, summed.shape[1])]
    return pl.pallas_call(
        fresh_kernel,
        grid_spec=pltpu.PrefetchScalarGridSpec(
            num_scalar_prefetch=2,
            grid=(1,),
            in_specs=[
                pl.BlockSpec(array.shape, lambda i, *_: (0, 0)) for array in (summed, cosine, sine)
            ],
            out_specs=[
                pl.BlockSpec(shape, lambda i, *_, n=len(shape): (0,) * n) for shape in shapes
            ],
        ),
        out_shape=[jax.ShapeDtypeStruct(shape, jnp.bfloat16) for shape in shapes],
    )(group, owner, summed, cosine, sine)


def place_pieces(group, length, holder_ref, slot_ref, refs, prefix_ref):
    pool_ref, main_ref, near_ref, two_ref, three_ref = refs
    ranks, _, block_rows, _ = pool_ref.shape
    rows = ranks * block_rows
    base = main_ref.shape[1]

    def one(index, counts):
        holder = holder_ref[group, index]
        distance = holder ^ group
        count = sum(jnp.where(distance == d, counts[d], 0) for d in range(4))
        at = pl.multiple_of(index * rows, rows)
        seen = index * rows < length

        @pl.when(jnp.logical_not(seen))
        def _():
            prefix_ref[pl.ds(at, rows), :] = jnp.zeros((rows, 2 * HD), jnp.bfloat16)

        @pl.when(seen & (distance == 0))
        def _():
            slot = slot_ref[group, index]
            for r in range(ranks):
                prefix_ref[pl.ds(at + r * block_rows, block_rows), :] = pool_ref[r, slot]

        low = count < base
        rest = count - base

        @pl.when(seen & (distance != 0) & low)
        def _():
            prefix_ref[pl.ds(at, rows), :] = main_ref[holder, count]

        def take(when, ref, n):
            @pl.when(seen & when)
            def _():
                prefix_ref[pl.ds(at, rows), :] = ref[n]

        take((distance == 1) & ~low, near_ref, rest)
        take((distance == 2) & ~low, two_ref, rest)
        take((distance == 3) & ~low, three_ref, rest)
        return tuple(n + (distance == d).astype(jnp.int32) for d, n in enumerate(counts))

    lax.fori_loop(0, holder_ref.shape[1], one, (jnp.int32(0),) * 4)


def attention_kernel(
    tile, ordered, length_ref, group_ref, rank_ref, holder_ref, slot_ref, q_ref, cos_ref, sin_ref, fresh_ref, *refs
):
    if ordered:
        *piece_refs, out_ref, prefix_ref = refs
    else:
        *piece_refs, weight_ref, send0, send1, keep0, keep1 = refs[:-5]
        prefix_ref, out_ref, rows_ref, held_ref, arrived = refs[-5:]
        fetch = pltpu.make_async_copy(weight_ref, held_ref, arrived)

        @pl.when(pl.program_id(0) == 0)
        def _():
            fetch.start()

    group = group_ref[0]
    span = prefix_ref.shape[0]
    row0 = pl.program_id(1) * tile

    @pl.when((pl.program_id(0) == 0) & (pl.program_id(1) == 0))
    def _():
        if ordered:
            prefix_ref[...] = piece_refs[0][...]
        else:
            place_pieces(group, length_ref[group], holder_ref, slot_ref, piece_refs, prefix_ref)

    seen = lax.broadcasted_iota(jnp.int32, (1, span), 1) < length_ref[group]
    bias = jnp.where(seen, 0.0, -1e30)
    columns = lax.broadcasted_iota(jnp.int32, (tile, fresh_ref.shape[0]), 1)
    rows = lax.broadcasted_iota(jnp.int32, (tile, fresh_ref.shape[0]), 0) + row0
    causal = columns <= rows
    cosine = cos_ref[pl.ds(pl.multiple_of(row0, tile), tile), :]
    sine = sin_ref[pl.ds(pl.multiple_of(row0, tile), tile), :]
    factor = HD ** (-0.5) * LOG2E

    def scores(query, keys):
        return lax.dot_general(
            query, keys, (((1,), (1,)), ((), ())), preferred_element_type=jnp.float32
        )

    for head in range(q_ref.shape[1] // HD):
        lanes = slice(head * HD, (head + 1) * HD)
        raw = q_ref[:, lanes]
        query = raw * cosine + pltpu.roll(raw, HD // 2, 1) * sine
        query = (query * factor).astype(jnp.bfloat16)
        old = scores(query, prefix_ref[:, :HD]) + bias
        new = jnp.where(causal, scores(query, fresh_ref[:, :HD]), -1e30)
        peak = jnp.maximum(
            jnp.max(old, axis=1, keepdims=True), jnp.max(new, axis=1, keepdims=True)
        )
        old, new = jnp.exp2(old - peak), jnp.exp2(new - peak)
        total = jnp.sum(old, axis=1, keepdims=True) + jnp.sum(new, axis=1, keepdims=True)
        mixed = jnp.dot(
            old.astype(jnp.bfloat16), prefix_ref[:, HD:], preferred_element_type=jnp.float32
        ) + jnp.dot(
            new.astype(jnp.bfloat16), fresh_ref[:, HD:], preferred_element_type=jnp.float32
        )
        mixed = (mixed / total).astype(jnp.bfloat16)
        if ordered:
            out_ref[:, lanes] = mixed
        else:
            out_ref[pl.program_id(0) * (q_ref.shape[1] // HD) + head] = mixed

    if not ordered:

        @pl.when(pl.program_id(0) == pl.num_programs(0) - 1)
        def _():
            fetch.wait()
            project_kernel(rank_ref[0], out_ref, rows_ref, held_ref, (send0, send1, keep0, keep1))


def project_kernel(rank, heads_ref, rows_ref, weight_ref, out_refs):
    quads, rows, width = out_refs[0].shape
    for head in range(heads_ref.shape[0]):
        for n in range(2 * quads):
            source = rank ^ (n % quads * 2) ^ (1 - n // quads)
            at = pl.multiple_of(source * rows, rows)
            rows_ref[n * rows : (n + 1) * rows, head * HD : (head + 1) * HD] = heads_ref[
                head, pl.ds(at, rows), :
            ]
    block = 1024
    for half in range(2):

        def one(step, carry, half=half):
            at = pl.multiple_of(step * block, block)
            source = pl.multiple_of(half * width + at, block)
            product = jnp.dot(
                rows_ref[...],
                weight_ref[:, pl.ds(source, block)],
                preferred_element_type=jnp.float32,
            ).astype(jnp.bfloat16)
            for n in range(quads):
                out_refs[half][n, :, pl.ds(at, block)] = product[n * rows : (n + 1) * rows]
                out_refs[2 + half][n, :, pl.ds(at, block)] = product[
                    (quads + n) * rows : (quads + n + 1) * rows
                ]
            return carry

        lax.fori_loop(0, width // block, one, 0)


def attention(
    prefix_len, group, rank, hit_holder, hit_slot, raw_queries, cosine, sine, fresh, pieces, w_out
):
    rows, width = raw_queries.shape
    tile = min(256, rows)
    span = hit_holder.shape[1] * BLK
    keys = span + rows
    ordered = w_out is None
    fixed = [cosine, sine, fresh, *pieces]

    def whole(array):
        return pl.BlockSpec(
            array.shape, lambda h, t, *_: (0,) * len(array.shape), pipeline_mode=pl.Buffered(1)
        )

    scratch = [pltpu.VMEM((span, 2 * HD), jnp.bfloat16)]
    in_specs = [pl.BlockSpec((tile, 2 * HD), lambda h, t, *_: (t, h))]
    in_specs += [whole(array) for array in fixed]
    if ordered:
        outs = [jax.ShapeDtypeStruct((rows, width), jnp.bfloat16)]
        out_specs = [pl.BlockSpec((tile, 2 * HD), lambda h, t, *_: (t, h))]
    else:
        fixed.append(w_out)
        in_specs.append(pl.BlockSpec(memory_space=pl.ANY))
        part = (4, rows // 8, w_out.shape[1] // 2)
        outs = [jax.ShapeDtypeStruct(part, jnp.bfloat16)] * 4
        out_specs = [pl.BlockSpec(part, lambda h, t, *_: (0, 0, 0))] * 4
        scratch += [
            pltpu.VMEM((width // HD, rows, HD), jnp.bfloat16),
            pltpu.VMEM((rows, width), jnp.bfloat16),
            pltpu.VMEM(w_out.shape, jnp.bfloat16),
            pltpu.SemaphoreType.DMA,
        ]
    return pl.pallas_call(
        functools.partial(attention_kernel, tile, ordered),
        grid_spec=pltpu.PrefetchScalarGridSpec(
            num_scalar_prefetch=5,
            grid=(width // (2 * HD), rows // tile),
            in_specs=in_specs,
            out_specs=out_specs,
            scratch_shapes=scratch,
        ),
        out_shape=outs,
        compiler_params=pltpu.CompilerParams(vmem_limit_bytes=44 * 1024 * 1024),
        cost_estimate=pl.CostEstimate(
            flops=4 * rows * width * keys,
            bytes_accessed=rows * width * 6,
            transcendentals=rows * width // HD * keys,
        ),
    )(prefix_len, group, rank, hit_holder, hit_slot, raw_queries, *fixed)


PAIRS = ((0, 2), (1, 3), (0, 3), (1, 2))


def pairs_wanted(prefix_len, hit_holder, base):
    requests, blocks = hit_holder.shape
    starts = jnp.arange(blocks, dtype=jnp.int32) * BLK
    seen = starts[None, :] < prefix_len[:, None]
    holders = jnp.arange(requests, dtype=jnp.int32)
    held = (hit_holder[:, None, :] == holders[None, :, None]) & seen[:, None, :]
    over = jnp.sum(held.astype(jnp.int32), axis=2) > base
    bits = [[0] * requests for _ in range(requests)]
    for n, (one, other) in enumerate(PAIRS):
        bits[one][other] = bits[other][one] = n + 1
    numbers = jnp.asarray(bits, jnp.int32)
    flags = [jnp.any(over & (numbers == n + 1)) for n in range(len(PAIRS))]
    return sum(flag.astype(jnp.int32) << n for n, flag in enumerate(flags))


def exchange_more(more, wanted, tokens, w_query):
    def branch(bits):
        def run(two, three, tokens, w_query):
            out = []
            for array, at in ((two, 0), (three, 2)):
                pairs = [PAIRS[n] for n in (at, at + 1) if bits >> n & 1]
                moves = [pair for one, other in pairs for pair in ((one, other), (other, one))]
                out.append(lax.ppermute(array, "req", moves) if moves else array)
            return (*out, query_project(tokens, w_query))

        return run

    return lax.switch(wanted, [branch(bits) for bits in range(16)], *more, tokens, w_query)


def query_kernel(tokens_ref, weight_ref, out_ref):
    out_ref[...] = jnp.dot(tokens_ref[...], weight_ref[...], preferred_element_type=jnp.float32)


def query_project(tokens, w_query):
    rows, depth = tokens.shape
    width = w_query.shape[1]
    block = 256
    return pl.pallas_call(
        query_kernel,
        grid=(width // block,),
        in_specs=[
            pl.BlockSpec((rows, depth), lambda i: (0, 0)),
            pl.BlockSpec((depth, block), lambda i: (0, i)),
        ],
        out_specs=pl.BlockSpec((rows, block), lambda i: (0, i)),
        out_shape=jax.ShapeDtypeStruct((rows, width), jnp.float32),
        compiler_params=pltpu.CompilerParams(vmem_limit_bytes=50 * 1024 * 1024),
        cost_estimate=pl.CostEstimate(flops=1024, bytes_accessed=1024, transcendentals=0),
    )(tokens, w_query)


def swap(array, bit):
    return lax.ppermute(array, "cp", [(i, i ^ bit) for i in range(8)])


def add(one, two):
    return one.astype(jnp.float32) + two.astype(jnp.float32)


VMEM_REF = pl.BlockSpec(memory_space=pltpu.VMEM)


def pair_kernel(near, keep_ref, got_ref, kept_ref, sent_ref):
    for n in range(2):
        stays, goes = (2 * n, 2 * n + 1) if near else (n, n + 2)
        kept_ref[n] = add(keep_ref[stays], got_ref[stays])
        sent_ref[n] = add(keep_ref[goes], got_ref[goes]).astype(sent_ref.dtype)


def pair_sum(keep, got, near):
    half = (2, *keep.shape[1:])
    outs = [jax.ShapeDtypeStruct(half, jnp.float32), jax.ShapeDtypeStruct(half, keep.dtype)]
    return pl.pallas_call(
        functools.partial(pair_kernel, near),
        in_specs=[VMEM_REF] * 2,
        out_specs=[VMEM_REF] * len(outs),
        out_shape=outs,
        compiler_params=pltpu.CompilerParams(vmem_limit_bytes=8 * 1024 * 1024),
    )(keep, got)


def level_kernel(kept_ref, got_ref, *refs):
    refs[-2][...] = add(kept_ref[0], got_ref[0])
    refs[-1][...] = add(kept_ref[1], got_ref[1]).astype(got_ref.dtype)
    if len(refs) > 2:
        refs[1][...] = refs[0][...]


def second_level(kept, sent, bit, *blocks):
    shape = kept.shape[1:]
    outs = [jax.ShapeDtypeStruct(array.shape, array.dtype) for array in blocks]
    outs += [jax.ShapeDtypeStruct(shape, jnp.float32), jax.ShapeDtypeStruct(shape, sent.dtype)]
    *blocks, kept, sent = pl.pallas_call(
        level_kernel,
        in_specs=[VMEM_REF] * (2 + len(blocks)),
        out_specs=[VMEM_REF] * len(outs),
        out_shape=outs,
        compiler_params=pltpu.CompilerParams(vmem_limit_bytes=8 * 1024 * 1024),
    )(kept, swap(sent, bit), *blocks)
    return *blocks, kept, swap(sent, 6 - bit)


def last_kernel(residual_ref, *refs):
    left, got_left, right, got_right, landed_ref, out_ref, cache_ref = refs
    half = left.shape[1]
    out_ref[0, :, :half] = (add(left[...], got_left[...]) + residual_ref[:, :half]).astype(
        jnp.bfloat16
    )
    out_ref[0, :, half:] = (add(right[...], got_right[...]) + residual_ref[:, half:]).astype(
        jnp.bfloat16
    )
    key_width = KVH * HD
    for source in range(cache_ref.shape[1]):
        for head in range(KVH):
            rows = landed_ref[source, head]
            at = head * HD
            cache_ref[0, source, :, at : at + HD] = rows[:, :HD]
            cache_ref[0, source, :, key_width + at : key_width + at + HD] = rows[:, HD:]


def last_sums(residual, left, right, landed, cache_shape):
    shapes = [(1, *residual.shape), cache_shape]
    return pl.pallas_call(
        last_kernel,
        grid=(1,),
        in_specs=[VMEM_REF] * 6,
        out_specs=[pl.BlockSpec(shape, lambda i, n=len(shape): (0,) * n) for shape in shapes],
        out_shape=[jax.ShapeDtypeStruct(shape, jnp.bfloat16) for shape in shapes],
        compiler_params=pltpu.CompilerParams(vmem_limit_bytes=12 * 1024 * 1024),
    )(residual, *left, *right, landed)


def local(
    hidden, residual, w_query, w_keyval, w_out, kv_pool, prefix_len, hit_holder, hit_slot, owner
):
    cp_count = lax.axis_size("cp")
    group_id = lax.axis_index("req")
    cp_rank = lax.axis_index("cp")
    tok_rows = hidden.shape[1]
    stretch_rows = tok_rows * cp_count
    slice_rows = w_keyval.shape[0]
    block_rows = kv_pool.shape[1]
    request_count = hit_holder.shape[0]
    prefix_blocks = hit_holder.shape[1]
    new_blocks = owner.shape[1]
    owner_cap = (new_blocks + 1) // 2
    holder_cap = prefix_blocks // 2
    heads_share = cp_count // KVH
    length = prefix_len[group_id]
    positions = length + jnp.arange(stretch_rows, dtype=jnp.int32)
    cosine, sine = rope_tables(positions)

    group = group_id.reshape(1)
    rank = cp_rank.reshape(1)
    fast = cp_count == 8 and request_count == 4 and owner_cap == 1 and block_rows % 16 == 0
    own = hidden[0]
    if fast:
        pool = lax.all_to_all(
            split_heads(kv_pool, own), "cp", split_axis=0, concat_axis=0, tiled=True
        )
        base = holder_cap // 2
        wanted = pairs_wanted(prefix_len, hit_holder, base)
        own, pool, cosine, sine, wanted = lax.optimization_barrier(
            (own, pool, cosine, sine, wanted)
        )
        packed = pack(
            group, rank, hit_holder, hit_slot, pool, w_keyval,
            kv_pool.shape[0], stretch_rows, holder_cap, base,
        )
        main, near, two_more, three_more, *terms = packed
        main = lax.all_to_all(main, "req", split_axis=0, concat_axis=0, tiled=True)
        near = lax.ppermute(near, "req", [(i, i ^ 1) for i in range(4)])
        send, keep = terms
        got = swap(send, 1)
        key_terms = second_level(*pair_sum(keep[..., :HD], got[..., :HD], True), 2)
        value_terms = second_level(*pair_sum(keep[..., HD:], got[..., HD:], False), 4)
        summed = jnp.concatenate([add(*key_terms), add(*value_terms)], axis=1)
        fresh, blocks = finish_fresh(group, owner, summed, cosine, sine, cp_count)
        gathered = lax.all_gather(own, "cp", axis=0, tiled=True)
        two, three, raw_queries = exchange_more((two_more, three_more), wanted, gathered, w_query)
        pieces = [pool, main, near, two, three]
    else:
        slot_ids = jnp.arange(holder_cap, dtype=jnp.int32)
        holds_hit = hit_holder == group_id
        hit_order = jnp.cumsum(holds_hit.astype(jnp.int32), axis=1) - 1
        picked = holds_hit[:, None, :] & (hit_order[:, None, :] == slot_ids[None, :, None])
        sources = jnp.sum(jnp.where(picked, hit_slot[:, None, :], 0), axis=2)
        by_head = kv_pool.reshape(-1, block_rows, 2, KVH, HD)[sources]
        by_head = jnp.transpose(by_head, (0, 4, 1, 2, 3, 5))
        sending = jnp.repeat(by_head, heads_share, axis=1).reshape(
            request_count * cp_count, holder_cap * block_rows, 2 * HD
        )
        arrived = lax.all_to_all(sending, ("req", "cp"), split_axis=0, concat_axis=0, tiled=True)
        arrived = arrived.reshape(request_count, cp_count, holder_cap, block_rows, 2 * HD)
        my_holders = hit_holder[group_id]
        hit_index = jnp.arange(prefix_blocks, dtype=jnp.int32)
        earlier = (my_holders[:, None] == my_holders[None, :]) & (
            hit_index[:, None] > hit_index[None, :]
        )
        hit_rank = jnp.sum(earlier.astype(jnp.int32), axis=1)
        pieces = [arrived[my_holders, :, hit_rank].reshape(prefix_blocks * BLK, 2 * HD)]

        gathered = lax.all_gather(own, "cp", axis=0, tiled=True)
        raw_queries = jnp.dot(gathered, w_query, preferred_element_type=jnp.float32)
        columns = lax.dynamic_slice_in_dim(gathered, cp_rank * slice_rows, slice_rows, 1)
        partial_kv = jnp.dot(columns, w_keyval, preferred_element_type=jnp.float32)
        partial_kv = jnp.transpose(
            partial_kv.reshape(stretch_rows, 2, KVH, HD), (2, 0, 1, 3)
        ).reshape(KVH, stretch_rows, 2 * HD)
        partial_kv = jnp.repeat(partial_kv, heads_share, axis=0)
        summed = lax.psum_scatter(partial_kv, "cp", scatter_dimension=0, tiled=True)[0]
        keys = summed[:, :HD]
        keys = keys * cosine + jnp.roll(keys, HD // 2, axis=1) * sine
        fresh = jnp.concatenate([keys, summed[:, HD:]], axis=1).astype(jnp.bfloat16)
    outs = attention(
        prefix_len, group, rank, hit_holder, hit_slot, raw_queries, cosine, sine, fresh, pieces,
        w_out if fast else None,
    )
    if fast:
        send0, send1, keep0, keep1 = outs
        blocks, *left = second_level(*pair_sum(keep0, swap(send0, 1), True), 2, blocks)
        right = second_level(*pair_sum(keep1, swap(send1, 1), False), 4)
        blocks = blocks.reshape(-1, *blocks.shape[2:])
        landed = lax.all_to_all(blocks, ("req", "cp"), split_axis=0, concat_axis=0, tiled=True)
        landed = landed.reshape(request_count, cp_count, block_rows, 2 * HD)
        cache_shape = (1, request_count, block_rows, 2 * KVH * HD)
        return tuple(last_sums(residual[0], left, right, landed, cache_shape))
    (attended,) = outs
    projected = lax.psum_scatter(
        jnp.dot(attended, w_out, preferred_element_type=jnp.float32).astype(jnp.bfloat16),
        "cp",
        scatter_dimension=0,
        tiled=True,
    ).astype(jnp.float32)
    layer_out = (residual[0].astype(jnp.float32) + projected).astype(jnp.bfloat16)[None]

    my_owners = owner[group_id]
    block_ids = jnp.arange(new_blocks, dtype=jnp.int32)
    before = (my_owners[:, None] == my_owners[None, :]) & (block_ids[:, None] > block_ids[None, :])
    owner_rank = jnp.sum(before.astype(jnp.int32), axis=1)
    targets = jnp.arange(request_count, dtype=jnp.int32)[:, None, None]
    cap_ids = jnp.arange(owner_cap, dtype=jnp.int32)[None, :, None]
    chosen = (my_owners[None, None, :] == targets) & (owner_rank[None, None, :] == cap_ids)
    block_pick = jnp.sum(jnp.where(chosen, block_ids[None, None, :], 0), axis=2)
    present = jnp.any(chosen, axis=2)
    blocks = fresh.reshape(new_blocks, cp_count, block_rows, 2 * HD)[block_pick]
    blocks = jnp.where(present[:, :, None, None, None], blocks, jnp.zeros((), jnp.bfloat16))
    blocks = jnp.transpose(blocks, (0, 2, 1, 3, 4)).reshape(
        request_count * cp_count, owner_cap * block_rows, 2 * HD
    )
    landed = lax.all_to_all(blocks, ("req", "cp"), split_axis=0, concat_axis=0, tiled=True)
    landed = landed.reshape(request_count, cp_count, owner_cap, block_rows, 2, HD)[:, ::heads_share]
    new_cache = jnp.transpose(landed, (0, 2, 3, 4, 1, 5)).reshape(
        1, request_count * owner_cap, block_rows, 2 * KVH * HD
    )
    return (layer_out, new_cache)


def solution(mesh):
    in_specs = (
        P("req", "cp", None),
        P("req", "cp", None),
        P(None, "cp"),
        P("cp", None),
        P("cp", None),
        P("req", "cp", None),
        P(),
        P(),
        P(),
        P(),
    )
    out_specs = (P("req", "cp", None), P("req", None, "cp", None))
    return jax.shard_map(local, mesh=mesh, in_specs=in_specs, out_specs=out_specs, check_vma=False)
```
